256 devices in a mesh: seq: 32 (over x, y, core), head: 8 (over z).
Axes of the slice: x: 4, y: 4, z: 8, core: 2. Of those that a mesh axis runs over, the one named last changes fastest.
Arguments:
- query_heads: bfloat16 [8192, 4096], P('seq', 'head'), may hold values from -6 to 6
- key_heads: bfloat16 [8192, 1024], P('seq', 'head'), may hold values from -6 to 6
- value_heads: bfloat16 [8192, 1024], P('seq', 'head'), may hold values from -6 to 6
- attention_out: bfloat16 [8192, 4096], P('seq', 'head'), may hold values from -6 to 6
- log_norm: float32 [32, 8192], P('head', 'seq'), as said below
- upstream: bfloat16 [8192, 4096], P('seq', 'head'), may hold values from -6 to 6
- output_weight: bfloat16 [4096, 4096], P('head'), may hold values from -0.09375 to 0.09375
- document_lengths: int32 [8], replicated, may hold values from 1 to 4096, as said below
- block_owners: int32 [64], replicated, may hold values from 0 to 63, each once
Outputs:
- query_grad: bfloat16 [8192, 4096], P('seq', 'head')
- key_grad: bfloat16 [8192, 1024], P('seq', 'head')
- value_grad: bfloat16 [8192, 1024], P('seq', 'head')
The draws below stay inside these ranges and needn't reach their ends.
Inputs may be any that keep to these rules, and one draw needn't show every extreme that they name: `document_lengths`: they sum to 8192; exactly one document has 4096 tokens. `block_owners`: A permutation: every row block is named once. log_norm[h, r] is the log of the sum over s with allowed(r, s) = 1 of exp(scores[h, r, s]).
All inputs are finite; a program needn't handle non-finite values.
Results may differ from the reference program's by a relative error of at most 0.013.
Values may be sent and summed in bfloat16 or wider, within the bound.
No kernel may reach another device: no remote copies, remote signals or barrier semaphores. Data moves between devices by JAX's collectives and lax.ppermute only.
A program may use at most 64 MiB of HBM per device.

```python
import math
import jax
import jax.numpy as jnp
from jax import lax

D = 4096
QH = 32
KVH = 8
HD = 128
TOK_DEV = 256
DOCS = 8
HALF = 128
TOKENS = 8192
MOST = 4096
N_SEQ = 32


def document_layout(key):
    key = jax.random.fold_in(key, 11)
    remainder = TOKENS - MOST
    shuffled = jax.random.permutation(jax.random.fold_in(key, 1), remainder - 1)
    cut_points = jnp.sort(shuffled[:DOCS - 2] + 1).astype(jnp.int32)
    boundaries = jnp.concatenate([jnp.zeros((1,), jnp.int32), cut_points, jnp.full((1,), remainder, jnp.int32)])
    pieces = boundaries[1:] - boundaries[:-1]
    placed = jax.random.randint(jax.random.fold_in(key, 2), (), 0, DOCS)
    document_index = jnp.arange(DOCS, dtype=jnp.int32)
    source = jnp.clip(document_index - (document_index > placed).astype(jnp.int32), 0, DOCS - 2)
    lengths = jnp.where(document_index == placed, MOST, pieces[source]).astype(jnp.int32)
    return lengths


def row_to_position(row_index):
    cycle_size = TOKENS // TOK_DEV
    row_block = row_index // HALF
    device = row_block // 2
    target = jnp.where(row_block % 2 == 0, device, 2 * cycle_size - 1 - device)
    return target * HALF + row_index % HALF


def base_queries(key):
    own_key = jax.random.fold_in(key, 3)
    return jnp.clip(jax.random.normal(own_key, (TOKENS, QH * HD), jnp.float32), -5.5, 5.5)


def base_keys(key):
    own_key = jax.random.fold_in(key, 5)
    return jnp.clip(jax.random.normal(own_key, (TOKENS, KVH * HD), jnp.float32), -5.5, 5.5)


def draw_document_lengths(key, part):
    lengths = document_layout(key)
    return lengths


def draw_query_heads(key, part):
    values = base_queries(key)
    return values.astype(jnp.bfloat16)


def draw_key_heads(key, part):
    values = base_keys(key)
    return values.astype(jnp.bfloat16)


def draw_log_norm(key, part):
    lengths = document_layout(key)
    query_values = base_queries(key)
    key_values = base_keys(key)
    group_size = QH // KVH
    queries = query_values.astype(jnp.bfloat16).astype(jnp.float32).reshape(TOKENS, KVH, group_size, HD)
    key_rows = key_values.astype(jnp.bfloat16).astype(jnp.float32).reshape(TOKENS, KVH, HD)
    positions_all = row_to_position(jnp.arange(TOKENS, dtype=jnp.int32))
    doc_ends = jnp.cumsum(lengths)
    documents = jnp.sum((doc_ends[None, :] <= positions_all[:, None]).astype(jnp.int32), axis=1)
    factor = 1.0 / math.sqrt(HD)

    def one_block(block_index):
        first_row = (block_index * HALF).astype(jnp.int32)
        query_block = lax.dynamic_slice_in_dim(queries, first_row, HALF, 0)
        query_pos = lax.dynamic_slice_in_dim(positions_all, first_row, HALF, 0)
        query_doc = lax.dynamic_slice_in_dim(documents, first_row, HALF, 0)
        allowed = (positions_all[None, :] <= query_pos[:, None]) & (documents[None, :] == query_doc[:, None])
        scores = jnp.einsum('qcgd,kcd->cgqk', query_block, key_rows, precision=lax.Precision.HIGHEST) * factor
        row_max = jnp.max(jnp.where(allowed, scores, -1e+30), axis=-1)
        totals = jnp.sum(jnp.where(allowed, jnp.exp(scores - row_max[..., None]), 0.0), axis=-1)
        return row_max + jnp.log(totals)
    blocks = lax.map(one_block, jnp.arange(TOKENS // HALF, dtype=jnp.int32))
    return jnp.transpose(blocks, (1, 2, 0, 3)).reshape(QH, TOKENS).astype(jnp.float32)


def shard_levels(key, dims, cuts, smallest, largest):
    loudness = 1.0
    for dim, shards_of in cuts:
        draws = jax.random.uniform(jax.random.fold_in(jax.random.fold_in(key, 6), dim), (shards_of,), jnp.float32, smallest / len(cuts), largest / len(cuts))
        loudness = loudness * jnp.repeat(jnp.exp(draws), dims[dim] // shards_of).reshape((-1,) + (1,) * (len(dims) - 1 - dim))
    return loudness


def noise(rng, extent, width, most, cuts=(), kind=jnp.bfloat16):
    values = jax.random.normal(rng, extent, jnp.float32) * width
    if len(cuts) > 0:
        values = shard_levels(rng, extent, cuts, -0.22, 0.18) * values
    return jnp.clip(values, min=-most, max=most).astype(kind)


def setup_inputs(seed: int = 0) -> dict:
    arg_keys = jax.random.split(jax.random.key(seed), 10)
    return {
        "query_heads": draw_query_heads(jax.random.fold_in(arg_keys[9], 71), 0),
        "key_heads": draw_key_heads(jax.random.fold_in(arg_keys[9], 71), 0),
        "value_heads": noise(arg_keys[2], (TOKENS, KVH * HD), 1.0, 6.0, ((0, 32), (1, 8))),
        "attention_out": noise(arg_keys[3], (TOKENS, QH * HD), 1.0, 6.0, ((0, 32), (1, 8))),
        "log_norm": draw_log_norm(jax.random.fold_in(arg_keys[9], 71), 0),
        "upstream": noise(arg_keys[5], (TOKENS, D), 1.0, 6.0, ((0, 32), (1, 8))),
        "output_weight": noise(arg_keys[6], (QH * HD, D), D ** -0.5, 0.09375, ((0, 8),)),
        "document_lengths": draw_document_lengths(jax.random.fold_in(arg_keys[9], 71), 0),
        "block_owners": jax.random.permutation(arg_keys[8], 2 * N_SEQ).astype(jnp.int32),
    }


def row_position(row_index, half_rows, cycle_size):
    row_block = row_index // half_rows
    device = row_block // 2
    target = jnp.where(row_block % 2 == 0, device, 2 * cycle_size - 1 - device)
    return target * half_rows + row_index % half_rows

def document_of(positions, document_lengths):
    doc_ends = jnp.cumsum(document_lengths)
    return lax.optimization_barrier(jnp.sum((doc_ends[None, :] <= positions[:, None]).astype(jnp.int32), axis=1))

def reference(query_heads, key_heads, value_heads, attention_out, log_norm, upstream, output_weight, document_lengths, block_owners):
    group_size = QH // KVH
    factor = 1.0 / math.sqrt(HD)
    out_grad = jnp.dot(upstream, output_weight.T, preferred_element_type=jnp.float32).astype(jnp.bfloat16)
    out_grad = lax.optimization_barrier(out_grad)
    positions = row_position(jnp.arange(TOKENS, dtype=jnp.int32), HALF, N_SEQ)
    documents = document_of(positions, document_lengths)
    queries = query_heads.reshape(TOKENS, KVH, group_size, HD).astype(jnp.float32)
    key_rows = key_heads.reshape(TOKENS, KVH, HD).astype(jnp.float32)
    value_rows = value_heads.reshape(TOKENS, KVH, HD).astype(jnp.float32)
    grad_rows = out_grad.reshape(TOKENS, KVH, group_size, HD).astype(jnp.float32)
    outputs = attention_out.reshape(TOKENS, KVH, group_size, HD).astype(jnp.float32)
    row_delta = lax.optimization_barrier(jnp.sum(grad_rows * outputs, axis=-1))
    norms = log_norm.reshape(KVH, group_size, TOKENS)

    def one_block(key_sums, block_index):
        first_row = (block_index * HALF).astype(jnp.int32)
        query_block = lax.dynamic_slice_in_dim(queries, first_row, HALF, 0)
        grad_block = lax.dynamic_slice_in_dim(grad_rows, first_row, HALF, 0)
        delta_block = jnp.transpose(lax.dynamic_slice_in_dim(row_delta, first_row, HALF, 0), (1, 2, 0))
        norm_block = lax.dynamic_slice_in_dim(norms, first_row, HALF, 2)
        query_pos = lax.dynamic_slice_in_dim(positions, first_row, HALF, 0)
        query_doc = lax.dynamic_slice_in_dim(documents, first_row, HALF, 0)
        allowed = (positions[None, :] <= query_pos[:, None]) & (documents[None, :] == query_doc[:, None])
        scores = jnp.einsum('qcgd,kcd->cgqk', query_block, key_rows) * factor
        weights = jnp.where(allowed, jnp.exp(scores - norm_block[..., None]), 0.0)
        weights_low = lax.optimization_barrier(weights.astype(jnp.bfloat16)).astype(jnp.float32)
        prob_grad = jnp.einsum('qcgd,kcd->cgqk', grad_block, value_rows)
        score_grad = weights * (prob_grad - delta_block[..., None])
        score_grad = lax.optimization_barrier(score_grad.astype(jnp.bfloat16)).astype(jnp.float32)
        query_part = jnp.einsum('cgqk,kcd->qcgd', score_grad, key_rows) * factor
        key_sum = key_sums[0] + jnp.einsum('cgqk,qcgd->kcd', score_grad, query_block) * factor
        value_sum = key_sums[1] + jnp.einsum('cgqk,qcgd->kcd', weights_low, grad_block)
        return ((key_sum, value_sum), query_part.astype(jnp.bfloat16))
    start_sums = (jnp.zeros((TOKENS, KVH, HD), jnp.float32), jnp.zeros((TOKENS, KVH, HD), jnp.float32))
    key_sums, query_parts = lax.scan(one_block, start_sums, jnp.arange(TOKENS // HALF, dtype=jnp.int32))
    query_grad = query_parts.reshape(TOKENS, QH * HD)
    key_all = key_sums[0].astype(jnp.bfloat16).reshape(2 * N_SEQ, HALF, KVH * HD)
    value_all = key_sums[1].astype(jnp.bfloat16).reshape(2 * N_SEQ, HALF, KVH * HD)
    key_grad = key_all[block_owners].reshape(TOKENS, KVH * HD)
    value_grad = value_all[block_owners].reshape(TOKENS, KVH * HD)
    return (query_grad, key_grad, value_grad)
```

```python
import functools
import math

import jax
import jax.numpy as jnp
from jax import lax
from jax.experimental import pallas as pl
from jax.experimental.pallas import tpu as pltpu
from jax.sharding import PartitionSpec as P

HD = 128
GROUP = 4
SIDE = 4
CHIPS = SIDE * SIDE
HEADS = 8
BLOCKS = 64
MINE = BLOCKS // 2
STACK = GROUP * HD
FACTOR = 1.0 / math.sqrt(HD)
LOG2E = math.log2(math.e)
VMEM_BYTES = 48 * 1024 * 1024

NT = (((1,), (1,)), ((), ()))
TN = (((0,), (0,)), ((), ()))
NN = (((1,), (0,)), ((), ()))

SWAP = [(i, i ^ 1) for i in range(2 * CHIPS)]
SAME_CORE = [[2 * c + k for c in range(CHIPS)] for k in range(2)]


def chip_shift(dx, dy):
    pairs = []
    for x in range(SIDE):
        for y in range(SIDE):
            target = ((x + dx) % SIDE) * SIDE + (y + dy) % SIDE
            for core in range(2):
                pairs.append(((x * SIDE + y) * 2 + core, target * 2 + core))
    return pairs


def head_shift(by):
    return [(i, (i + by) % HEADS) for i in range(HEADS)]


def swapped(value):
    return lax.ppermute(value, "seq", SWAP)


def vmem():
    return pl.BlockSpec(memory_space=pltpu.VMEM)


def smem():
    return pl.BlockSpec(memory_space=pltpu.SMEM)


def project_first(u0, u1, u2, u3, u4, w0, w1, w2, w3, w4, total_ref):
    total = lax.dot_general(u0[...], w0[...], NT, preferred_element_type=jnp.float32)
    for u, w in ((u1, w1), (u2, w2), (u3, w3), (u4, w4)):
        total += lax.dot_general(u[...], w[...], NT, preferred_element_type=jnp.float32)
    total_ref[...] = total


def project_last(total_ref, u5, u6, top, bottom, w5, w6, w7, attention_ref, grad_ref, delta_ref):
    for slot, far in ((0, top), (1, bottom)):
        rows = slice(slot * HD, (slot + 1) * HD)
        total = total_ref[rows, :]
        total += lax.dot_general(u5[rows, :], w5[...], NT, preferred_element_type=jnp.float32)
        total += lax.dot_general(u6[rows, :], w6[...], NT, preferred_element_type=jnp.float32)
        total += lax.dot_general(far[...], w7[...], NT, preferred_element_type=jnp.float32)
        grad = total.astype(jnp.bfloat16)
        products = grad.astype(jnp.float32) * attention_ref[rows, :].astype(jnp.float32)
        for g in range(GROUP):
            columns = slice(g * HD, (g + 1) * HD)
            grad_ref[slot * STACK + g * HD : slot * STACK + (g + 1) * HD, :] = grad[:, columns]
            delta_ref[slot, :, columns] = jnp.sum(
                jnp.transpose(products[:, columns]), axis=0, keepdims=True
            )


def sort_keys(source_ref, keys_ref, values_ref, sorted_keys, sorted_values):
    def move(n, carry):
        source = pl.multiple_of(source_ref[0, n] * HD, HD)
        target = pl.multiple_of(n * HD, HD)
        sorted_keys[pl.ds(target, HD), :] = keys_ref[pl.ds(source, HD), :]
        source = pl.multiple_of(source_ref[1, n] * HD, HD)
        sorted_values[pl.ds(target, HD), :] = values_ref[pl.ds(source, HD), :]
        return carry

    lax.fori_loop(0, MINE, move, 0)
    sorted_keys[MINE * HD :, :] = jnp.zeros((HD, HD), jnp.bfloat16)
    sorted_values[MINE * HD :, :] = jnp.zeros((HD, HD), jnp.bfloat16)


def attend(
    position_ref,
    slot_ref,
    bound_ref,
    keys_ref,
    values_ref,
    q_own,
    q_sib,
    do_own,
    do_sib,
    norm_ref,
    first_ref,
    last_ref,
    delta_own,
    delta_sib,
    parts_ref,
    dq_own,
    dq_sib,
    dk_ref,
    dv_ref,
    dqt_ref,
):
    dk_ref[...] = jnp.zeros_like(dk_ref)
    dv_ref[...] = jnp.zeros_like(dv_ref)
    upper = lax.broadcasted_iota(jnp.int32, (2 * HD, 1), 0)
    for block in range(4):
        q_ref, do_ref, delta_ref, dq_ref = (
            (q_own, do_own, delta_own, dq_own),
            (q_sib, do_sib, delta_sib, dq_sib),
        )[block // 2]
        slot = block % 2
        rows = slice(slot * STACK, (slot + 1) * STACK)
        norm = norm_ref[block]
        first = first_ref[block]
        last = last_ref[block]
        delta = delta_ref[slot]
        begin = bound_ref[2 * block]
        end = bound_ref[2 * block + 1]
        dqt_ref[...] = jnp.zeros_like(dqt_ref)

        def visit(step, carry):
            index = begin + 2 * step
            here = pl.ds(pl.multiple_of(index * HD, HD), 2 * HD)
            queries = q_ref[rows, :]
            grads = do_ref[rows, :]
            keys = keys_ref[here, :]
            scores = lax.dot_general(keys, queries, NT, preferred_element_type=jnp.float32)
            prob_grad = lax.dot_general(
                values_ref[here, :], grads, NT, preferred_element_type=jnp.float32
            )
            low = position_ref[index] * HD
            high = (position_ref[index + 1] - 1) * HD
            place = upper + jnp.where(upper < HD, low, high)
            allowed = (place >= first) & (place <= last)
            weights = jnp.where(allowed, jnp.exp2(scores * (FACTOR * LOG2E) - norm), 0.0)
            score_grad = (weights * (prob_grad - delta)).astype(jnp.bfloat16)
            dv_ref[here, :] += lax.dot_general(
                weights.astype(jnp.bfloat16), grads, NN, preferred_element_type=jnp.float32
            )
            dk_ref[here, :] += lax.dot_general(
                score_grad, queries, NN, preferred_element_type=jnp.float32
            )
            dqt_ref[...] += lax.dot_general(
                keys, score_grad, TN, preferred_element_type=jnp.float32
            )
            return carry

        lax.fori_loop(0, (end - begin + 1) // 2, visit, 0)
        for g in range(GROUP):
            columns = slice(g * HD, (g + 1) * HD)
            dq_ref[slot * HD : (slot + 1) * HD, columns] = (
                jnp.transpose(dqt_ref[:, columns]) * FACTOR
            )

    def hand_out(n, carry):
        source = pl.ds(pl.multiple_of(n * HD, HD), HD)
        target = pl.ds(pl.multiple_of(slot_ref[n] * HD, HD), HD)
        parts_ref[target, :HD] = (dk_ref[source, :] * FACTOR).astype(jnp.bfloat16)
        parts_ref[target, HD:] = dv_ref[source, :].astype(jnp.bfloat16)
        return carry

    lax.fori_loop(0, MINE, hand_out, 0)


def gather_chips(value, first, second):
    step = lambda axis, by: chip_shift(by, 0) if axis == "x" else chip_shift(0, by)
    near = [value] + [lax.ppermute(value, "seq", step(first, by)) for by in (1, 2, 3)]
    bundle = jnp.concatenate(near, axis=0)
    return [bundle] + [lax.ppermute(bundle, "seq", step(second, by)) for by in (1, 2, 3)]


def per_device(
    query_heads,
    key_heads,
    value_heads,
    attention_out,
    log_norm,
    upstream,
    output_weight,
    document_lengths,
    block_owners,
):
    me = lax.axis_index("seq")
    my_head = lax.axis_index("head")
    core = me % 2
    my_x = me // (2 * SIDE)
    my_y = (me // 2) % SIDE
    width = upstream.shape[1]

    forth, back = [upstream], [upstream]
    for _ in range(3):
        forth.append(lax.ppermute(forth[-1], "head", head_shift(1)))
        back.append(lax.ppermute(back[-1], "head", head_shift(-1)))
    top = lax.ppermute(forth[3][:HD], "head", head_shift(1))
    bottom = lax.ppermute(back[3][HD:], "head", head_shift(-1))

    def weight_of(offset):
        source = (my_head + offset) % HEADS
        return lax.dynamic_slice_in_dim(output_weight, source * width, width, 1)

    own_keys = gather_chips(key_heads, "y", "x")
    own_values = gather_chips(value_heads, "x", "y")
    keys_all = jnp.concatenate(own_keys + [swapped(v) for v in own_keys], axis=0)
    values_all = jnp.concatenate(own_values + [swapped(v) for v in own_values], axis=0)

    places = jnp.arange(BLOCKS, dtype=jnp.int32)
    row_block = jnp.where(places < MINE, 2 * places, 2 * (BLOCKS - 1 - places) + 1)
    target = jnp.sum(
        jnp.where(block_owners[None, :] == row_block[:, None], places[None, :], 0), axis=1
    )
    mine = (target // 2) % 2 == core
    rank = jnp.sum(
        (mine[None, :] & (places[None, :] < places[:, None])).astype(jnp.int32), axis=1
    )
    listed = mine[None, :] & (rank[None, :] == places[:MINE, None])

    def pick(values):
        return jnp.sum(jnp.where(listed, values[None, :], 0), axis=1)

    positions = pick(places)
    slots = pick((target // 4) * 2 + target % 2)
    chip = row_block // 4
    steps_x = (my_x - chip // SIDE) % SIDE
    steps_y = (my_y - chip % SIDE) % SIDE
    far_core = jnp.where((row_block // 2) % 2 == core, 0, MINE)
    sources = jnp.stack(
        [
            pick(far_core + (steps_x * SIDE + steps_y) * 2 + row_block % 2),
            pick(far_core + (steps_y * SIDE + steps_x) * 2 + row_block % 2),
        ]
    )
    sibling = me ^ 1
    query_blocks = jnp.stack([me, BLOCKS - 1 - me, sibling, BLOCKS - 1 - sibling])
    last = query_blocks[:, None] * HD + jnp.arange(HD, dtype=jnp.int32)[None, :]
    ends = jnp.cumsum(document_lengths)
    first = jnp.max(
        jnp.where(ends[None, None, :] <= last[:, :, None], ends[None, None, :], 0), axis=2
    )
    begin = jnp.sum((positions[None, :] < first[:, :1] // HD).astype(jnp.int32), axis=1)
    end = jnp.sum((positions[None, :] <= query_blocks[:, None]).astype(jnp.int32), axis=1)
    bounds = jnp.stack([begin, end], axis=1).reshape(8)
    padded = jnp.concatenate([positions, jnp.full((8,), 4 * BLOCKS, jnp.int32)])
    first = jnp.tile(first, (1, GROUP)).reshape(4, 1, STACK)
    last = jnp.tile(last, (1, GROUP)).reshape(4, 1, STACK)

    sorted_shape = jax.ShapeDtypeStruct(((MINE + 1) * HD, HD), jnp.bfloat16)
    keys, values = pl.pallas_call(
        sort_keys,
        out_shape=(sorted_shape, sorted_shape),
        in_specs=[smem(), vmem(), vmem()],
        out_specs=(vmem(), vmem()),
        compiler_params=pltpu.CompilerParams(vmem_limit_bytes=VMEM_BYTES),
        cost_estimate=pl.CostEstimate(flops=0, bytes_accessed=6 << 20, transcendentals=0),
        name="sort_keys",
    )(sources, keys_all, values_all)

    queries = (
        query_heads.reshape(2, HD, GROUP, HD).transpose(0, 2, 1, 3).reshape(2 * STACK, HD)
    )
    queries_sib = swapped(queries)
    norms = jnp.concatenate([log_norm, swapped(log_norm)], axis=1)
    norms = (norms * LOG2E).reshape(GROUP, 4, HD).transpose(1, 0, 2).reshape(4, 1, STACK)

    tokens = upstream.shape[0]
    total = pl.pallas_call(
        project_first,
        out_shape=jax.ShapeDtypeStruct((tokens, STACK), jnp.float32),
        in_specs=[vmem()] * 10,
        out_specs=vmem(),
        compiler_params=pltpu.CompilerParams(vmem_limit_bytes=VMEM_BYTES),
        cost_estimate=pl.CostEstimate(
            flops=2 * tokens * 5 * width * STACK, bytes_accessed=4 << 20, transcendentals=0
        ),
        name="project_first",
    )(
        upstream, forth[1], back[1], forth[2], back[2],
        *[weight_of(offset) for offset in (0, -1, 1, -2, 2)],
    )
    grads, delta = pl.pallas_call(
        project_last,
        out_shape=(
            jax.ShapeDtypeStruct((2 * STACK, HD), jnp.bfloat16),
            jax.ShapeDtypeStruct((2, 1, STACK), jnp.float32),
        ),
        in_specs=[vmem()] * 9,
        out_specs=(vmem(), vmem()),
        compiler_params=pltpu.CompilerParams(vmem_limit_bytes=VMEM_BYTES),
        cost_estimate=pl.CostEstimate(
            flops=2 * tokens * 3 * width * STACK, bytes_accessed=3 << 20, transcendentals=0
        ),
        name="project_last",
    )(
        total, forth[3], back[3], top, bottom,
        *[weight_of(offset) for offset in (-3, 3, 4)], attention_out,
    )
    grads_sib = swapped(grads)
    delta_sib = swapped(delta)

    parts, dq_own, dq_sib = pl.pallas_call(
        attend,
        out_shape=(
            jax.ShapeDtypeStruct((MINE * HD, 2 * HD), jnp.bfloat16),
            jax.ShapeDtypeStruct((tokens, STACK), jnp.float32),
            jax.ShapeDtypeStruct((tokens, STACK), jnp.float32),
        ),
        in_specs=[smem()] * 3 + [vmem()] * 11,
        out_specs=(vmem(), vmem(), vmem()),
        scratch_shapes=[
            pltpu.VMEM(((MINE + 1) * HD, HD), jnp.float32),
            pltpu.VMEM(((MINE + 1) * HD, HD), jnp.float32),
            pltpu.VMEM((HD, STACK), jnp.float32),
        ],
        compiler_params=pltpu.CompilerParams(vmem_limit_bytes=VMEM_BYTES),
        cost_estimate=pl.CostEstimate(
            flops=35 * 10 * GROUP * HD**3, bytes_accessed=8 << 20, transcendentals=0
        ),
        name="attend",
    )(
        padded, slots, bounds, keys, values, queries, queries_sib, grads, grads_sib,
        norms, first, last, delta, delta_sib,
    )
    query_grad = (dq_own + swapped(dq_sib)).astype(jnp.bfloat16)
    received = lax.all_to_all(
        parts.reshape(CHIPS, 2 * HD, 2 * HD), "seq", 0, 0, tiled=True,
        axis_index_groups=SAME_CORE,
    )
    finished = jnp.sum(received.astype(jnp.float32), axis=0).astype(jnp.bfloat16)
    return (query_grad, finished[:, :HD], finished[:, HD:])


def solution(mesh):
    placed = (
        P("seq", "head"),
        P("seq", "head"),
        P("seq", "head"),
        P("seq", "head"),
        P("head", "seq"),
        P("seq", "head"),
        P("head", None),
        P(),
        P(),
    )
    return jax.shard_map(
        per_device,
        mesh=mesh,
        in_specs=placed,
        out_specs=(P("seq", "head"), P("seq", "head"), P("seq", "head")),
        check_vma=False,
    )
```

```python
import math

import jax
import jax.numpy as jnp
from jax import lax
from jax.experimental import pallas as pl
from jax.experimental.pallas import tpu as pltpu
from jax.sharding import PartitionSpec as P

HD = 128
GROUP = 4
SIDE = 4
CHIPS = SIDE * SIDE
HEADS = 8
BLOCKS = 64
MINE = BLOCKS // 2
STACK = GROUP * HD
FACTOR = 1.0 / math.sqrt(HD)
LOG2E = math.log2(math.e)

NT = (((1,), (1,)), ((), ()))
TN = (((0,), (0,)), ((), ()))
NN = (((1,), (0,)), ((), ()))

SWAP = [(i, i ^ 1) for i in range(2 * CHIPS)]
SAME_CORE = [[2 * c + k for c in range(CHIPS)] for k in range(2)]


def chip_shift(dx, dy):
    pairs = []
    for x in range(SIDE):
        for y in range(SIDE):
            target = ((x + dx) % SIDE) * SIDE + (y + dy) % SIDE
            for core in range(2):
                pairs.append(((x * SIDE + y) * 2 + core, target * 2 + core))
    return pairs


def head_shift(by):
    return [(i, (i + by) % HEADS) for i in range(HEADS)]


def swapped(value):
    return lax.ppermute(value, "seq", SWAP)


def vmem():
    return pl.BlockSpec(memory_space=pltpu.VMEM)


def smem():
    return pl.BlockSpec(memory_space=pltpu.SMEM)


def project_first(_bound, own, forth_1, back_1, forth_2, back_2, weight, total_ref, later_ref, held, sems):
    me = lax.axis_index("head")
    depth = held.shape[2]
    offsets = (0, -1, 1, -2, 2, -3, 3, 4)

    def fetch(n):
        source = lax.rem(me + offsets[n] + HEADS, HEADS)
        columns = pl.ds(pl.multiple_of(source * depth, depth), depth)
        target = held.at[n] if n < 5 else later_ref.at[n - 5]
        return pltpu.make_async_copy(weight.at[:, columns], target, sems.at[n])

    for n in range(8):
        fetch(n).start()
    total = jnp.zeros(total_ref.shape, jnp.float32)
    for n, rows in enumerate((own, forth_1, back_1, forth_2, back_2)):
        fetch(n).wait()
        total += lax.dot_general(rows[...], held[n], NT, preferred_element_type=jnp.float32)
    total_ref[...] = total
    for n in range(5, 8):
        fetch(n).wait()


def project_last(total_ref, forth_3, back_3, top, bottom, weight, attention_ref, grad_ref, delta_ref):
    for slot, far in ((0, top), (1, bottom)):
        rows = slice(slot * HD, (slot + 1) * HD)
        total = total_ref[rows, :]
        for n, part in enumerate((forth_3[rows, :], back_3[rows, :], far[...])):
            total += lax.dot_general(part, weight[n], NT, preferred_element_type=jnp.float32)
        grad = total.astype(jnp.bfloat16)
        products = grad.astype(jnp.float32) * attention_ref[rows, :].astype(jnp.float32)
        for g in range(GROUP):
            columns = slice(g * HD, (g + 1) * HD)
            grad_ref[slot * STACK + g * HD : slot * STACK + (g + 1) * HD, :] = grad[:, columns]
            delta_ref[slot, :, columns] = jnp.sum(
                jnp.transpose(products[:, columns]), axis=0, keepdims=True
            )


def plan(lengths, owners, position, slot, bound, place, target, before):
    me = lax.axis_index("seq")
    core = me & 1
    my_x, my_y = me >> 3, (me >> 1) & 3

    def invert(i, carry):
        target[owners[i]] = i
        return carry

    lax.fori_loop(0, BLOCKS, invert, 0, unroll=8)

    def visit(t, n):
        row = jnp.where(t < MINE, 2 * t, 2 * (BLOCKS - 1 - t) + 1)
        goal = target[row]
        mine = ((goal >> 1) & 1) == core
        before[t] = n
        position[n] = t
        slot[n] = (goal >> 2) * 2 + (goal & 1)
        far = jnp.where(((row >> 1) & 1) == core, 0, MINE)
        back_x = (my_x - (row >> 4) + SIDE) & 3
        back_y = (my_y - ((row >> 2) & 3) + SIDE) & 3
        place[far + back_x * 8 + back_y * 2 + (row & 1)] = jnp.where(mine, n, MINE)
        return n + mine.astype(jnp.int32)

    before[BLOCKS] = lax.fori_loop(0, BLOCKS, visit, jnp.int32(0), unroll=8)
    position[MINE] = 4 * BLOCKS
    for q, top in enumerate((me, BLOCKS - 1 - me, me ^ 1, BLOCKS - 1 - (me ^ 1))):
        end = start = jnp.int32(0)
        for d in range(lengths.shape[0]):
            end = end + lengths[d]
            start = jnp.where(end <= top * HD, end, start)
        bound[2 * q] = before[start >> 7]
        bound[2 * q + 1] = before[top + 1]


def tip(forth, back, top, bottom):
    top[...] = forth[:HD, :]
    bottom[...] = back[HD:, :]


def join(*refs):
    rows = refs[0].shape[0]
    for n in range(SIDE):
        refs[-1][n * rows : (n + 1) * rows, :] = refs[n][...]


def halve(forth, back, *refs):
    rows = refs[-1].shape[0]
    refs[-2][...] = forth[:rows, :]
    refs[-1][...] = back[rows:, :]


def sort_keys(place, *refs):
    pieces, (sorted_keys, sorted_values) = refs[:-2], refs[-2:]
    firsts = [side + first for side in (0, MINE) for first in (0, 8, 24, 16, 20)]
    goals = [place[n] for n in range(BLOCKS)]
    for first, piece in zip(firsts, pieces):
        for n in range(piece.shape[0] // HD):
            goal = pl.ds(pl.multiple_of(goals[first + n] * HD, HD), HD)
            rows = slice(n * HD, (n + 1) * HD)
            sorted_keys[goal, :] = piece[rows, :HD]
            sorted_values[goal, :] = piece[rows, HD:]
    for out in (sorted_keys, sorted_values):
        out[MINE * HD :, :] = jnp.zeros((HD, HD), jnp.bfloat16)


def attend(
    lengths,
    position_ref,
    slot_ref,
    bound_ref,
    keys_ref,
    values_ref,
    q_own,
    q_sib,
    do_own,
    do_sib,
    norm_own,
    norm_sib,
    delta_own,
    delta_sib,
    parts_ref,
    dq_own,
    dq_sib,
    dk_ref,
    dv_ref,
    dqt_ref,
    q_ref,
    do_ref,
):
    me = lax.axis_index("seq")
    dk_ref[...] = jnp.zeros_like(dk_ref)
    dv_ref[...] = jnp.zeros_like(dv_ref)
    upper = lax.broadcasted_iota(jnp.int32, (2 * HD, 1), 0)
    lane = lax.broadcasted_iota(jnp.int32, (1, 2 * STACK), 1)
    for slot in range(2):
        rows = slice(slot * HD, (slot + 1) * HD)
        for side, (queries, grads) in enumerate(((q_own, do_own), (q_sib, do_sib))):
            for g in range(GROUP):
                at = side * STACK + g * HD
                q_ref[at : at + HD, :] = queries[rows, g * HD : (g + 1) * HD]
            do_ref[side * STACK : (side + 1) * STACK, :] = grads[slot * STACK : (slot + 1) * STACK, :]
        norm = LOG2E * jnp.concatenate(
            [norms[g : g + 1, rows] for norms in (norm_own, norm_sib) for g in range(GROUP)], axis=1
        )
        delta = jnp.concatenate([delta_own[slot], delta_sib[slot]], axis=1)
        tops = [other if slot == 0 else BLOCKS - 1 - other for other in (me, me ^ 1)]
        last = jnp.where(lane < STACK, tops[0] * HD, tops[1] * HD) + (lane & (HD - 1))
        end = jnp.int32(0)
        first = jnp.zeros_like(last)
        for d in range(lengths.shape[0]):
            end = end + lengths[d]
            first = jnp.where(end <= last, end, first)
        begin = jnp.minimum(bound_ref[2 * slot], bound_ref[2 * slot + 4])
        stop = jnp.maximum(bound_ref[2 * slot + 1], bound_ref[2 * slot + 5])
        dqt_ref[...] = jnp.zeros_like(dqt_ref)

        def visit(step, carry):
            index = begin + 2 * step
            here = pl.ds(pl.multiple_of(index * HD, HD), 2 * HD)
            keys = keys_ref[here, :]
            queries = q_ref[...]
            grads = do_ref[...]
            low = position_ref[index] * HD
            high = (position_ref[index + 1] - 1) * HD
            place = upper + jnp.where(upper < HD, low, high)
            scores = lax.dot_general(keys, queries, NT, preferred_element_type=jnp.float32)
            prob_grad = lax.dot_general(
                values_ref[here, :], grads, NT, preferred_element_type=jnp.float32
            )
            allowed = (place >= first) & (place <= last)
            weights = jnp.where(allowed, jnp.exp2(scores * (FACTOR * LOG2E) - norm), 0.0)
            score_grad = (weights * (prob_grad - delta)).astype(jnp.bfloat16)
            dv_ref[here, :] += lax.dot_general(
                weights.astype(jnp.bfloat16), grads, NN, preferred_element_type=jnp.float32
            )
            dk_ref[here, :] += lax.dot_general(
                score_grad, queries, NN, preferred_element_type=jnp.float32
            )
            dqt_ref[...] += lax.dot_general(
                keys, score_grad, TN, preferred_element_type=jnp.float32
            )
            return carry

        lax.fori_loop(0, (stop - begin + 1) >> 1, visit, 0)
        for side, out in enumerate((dq_own, dq_sib)):
            for g in range(GROUP):
                at = side * STACK + g * HD
                out[rows, g * HD : (g + 1) * HD] = (
                    jnp.transpose(dqt_ref[:, at : at + HD]) * FACTOR
                )

    def hand_out(n, carry):
        source = pl.ds(pl.multiple_of(n * HD, HD), HD)
        target = pl.ds(pl.multiple_of(slot_ref[n] * HD, HD), HD)
        parts_ref[target, :HD] = (dk_ref[source, :] * FACTOR).astype(jnp.bfloat16)
        parts_ref[target, HD:] = dv_ref[source, :].astype(jnp.bfloat16)
        return carry

    lax.fori_loop(0, MINE, hand_out, 0, unroll=2)


def anywhere():
    return pl.BlockSpec(memory_space=pl.ANY)


def array(shape, dtype):
    return jax.ShapeDtypeStruct(shape, dtype)


def call(body, outs, ins, out_specs, flops, moved, scratch=(), room=16):
    return pl.pallas_call(
        body,
        out_shape=outs,
        in_specs=ins,
        out_specs=out_specs,
        scratch_shapes=scratch,
        compiler_params=pltpu.CompilerParams(vmem_limit_bytes=room << 20),
        cost_estimate=pl.CostEstimate(flops=flops, bytes_accessed=moved, transcendentals=0),
        name=body.__name__,
    )


def per_device(
    query_heads,
    key_heads,
    value_heads,
    attention_out,
    log_norm,
    upstream,
    output_weight,
    document_lengths,
    block_owners,
):
    tokens, width = upstream.shape
    bf16, f32, i32 = jnp.bfloat16, jnp.float32, jnp.int32

    def along(axis, value, by):
        if axis == "z":
            return lax.ppermute(value, "head", head_shift(by))
        return lax.ppermute(value, "seq", chip_shift(by, 0) if axis == "x" else chip_shift(0, by))

    position, slot, bound, place = call(
        plan,
        (array((40,), i32), array((40,), i32), array((8,), i32), array((64,), i32)),
        [smem()] * 2,
        [smem()] * 4,
        0,
        1 << 20,
        [pltpu.SMEM((BLOCKS,), i32), pltpu.SMEM((BLOCKS + 8,), i32)],
    )(document_lengths, block_owners)

    pair = jnp.concatenate([key_heads, value_heads], axis=1)
    near = [pair, *[along("y", pair, by) for by in (1, 3, 2)]]
    forth, back = [upstream], [upstream]
    for _ in range(3):
        forth.append(along("z", forth[-1], 1))
        back.append(along("z", back[-1], -1))
    q_sib, norm_sib = swapped(query_heads), swapped(log_norm)

    bundle_0 = call(
        join,
        array((SIDE * tokens, 2 * HD), bf16),
        [vmem()] * 4 + [smem()],
        vmem(),
        30_000_000_000,
        1 << 20,
    )(near[0], near[1], near[3], near[2], bound)
    bundle_1, bundle_3 = along("x", bundle_0, 1), along("x", bundle_0, -1)

    total, later = call(
        project_first,
        (array((tokens, STACK), f32), array((3, STACK, width), bf16)),
        [smem()] + [vmem()] * 5 + [anywhere()],
        [vmem()] * 2,
        10_000_000_000,
        6 << 20,
        [pltpu.VMEM((5, STACK, width), bf16), pltpu.SemaphoreType.DMA((8,))],
    )(bound, upstream, forth[1], back[1], forth[2], back[2], output_weight)

    half = array((SIDE * tokens // 2, 2 * HD), bf16)
    halves = call(
        halve, (half, half), [vmem()] * 2, [vmem()] * 2, 30_000_000_000, 1 << 20
    )(bundle_1, bundle_3)
    pieces = [bundle_0, bundle_1, bundle_3, along("x", halves[0], 1), along("x", halves[1], -1)]

    quarter = array((tokens // 2, width), bf16)
    tips = call(
        tip, (quarter, quarter), [vmem()] * 2, [vmem()] * 2, 0, 1 << 20
    )(forth[3], back[3])
    top, bottom = along("z", tips[0], 1), along("z", tips[1], -1)
    grads, delta = call(
        project_last,
        (array((2 * STACK, HD), bf16), array((2, 1, STACK), f32)),
        [vmem()] * 7,
        [vmem()] * 2,
        2 * tokens * 3 * width * STACK,
        3 << 20,
    )(total, forth[3], back[3], top, bottom, later, attention_out)

    in_order = array(((MINE + 1) * HD, HD), bf16)
    keys, values = call(
        sort_keys, (in_order, in_order), [smem()] + [vmem()] * 10, [vmem()] * 2, 0, 6 << 20
    )(place, *pieces, *map(swapped, pieces))

    parts, dq_own, dq_sib = call(
        attend,
        (array((MINE * HD, 2 * HD), bf16), array((tokens, STACK), f32), array((tokens, STACK), f32)),
        [smem()] * 4 + [vmem()] * 10,
        [vmem()] * 3,
        35 * 10 * GROUP * HD**3,
        8 << 20,
        [
            pltpu.VMEM(((MINE + 1) * HD, HD), f32),
            pltpu.VMEM(((MINE + 1) * HD, HD), f32),
            pltpu.VMEM((HD, 2 * STACK), f32),
            pltpu.VMEM((2 * STACK, HD), bf16),
            pltpu.VMEM((2 * STACK, HD), bf16),
        ],
        28,
    )(
        document_lengths, position, slot, bound, keys, values, query_heads, q_sib,
        grads, swapped(grads), log_norm, norm_sib, delta, swapped(delta),
    )
    query_grad = (dq_own + swapped(dq_sib)).astype(bf16)
    received = lax.all_to_all(
        parts.reshape(CHIPS, 2 * HD, 2 * HD), "seq", 0, 0, tiled=True,
        axis_index_groups=SAME_CORE,
    )
    finished = jnp.sum(received.astype(f32), axis=0).astype(bf16)
    return (query_grad, finished[:, :HD], finished[:, HD:])


def solution(mesh):
    placed = (
        P("seq", "head"),
        P("seq", "head"),
        P("seq", "head"),
        P("seq", "head"),
        P("head", "seq"),
        P("seq", "head"),
        P("head", None),
        P(),
        P(),
    )
    return jax.shard_map(
        per_device,
        mesh=mesh,
        in_specs=placed,
        out_specs=(P("seq", "head"), P("seq", "head"), P("seq", "head")),
        check_vma=False,
    )
```

```python
import math

import jax
import jax.numpy as jnp
from jax import lax
from jax.experimental import pallas as pl
from jax.experimental.pallas import tpu as pltpu
from jax.sharding import PartitionSpec as P

HD = 128
GROUP = 4
SIDE = 4
CHIPS = SIDE * SIDE
HEADS = 8
BLOCKS = 64
SIDE_BLOCKS = BLOCKS // 2
MINE = BLOCKS // 4
STACK = GROUP * HD
FACTOR = 1.0 / math.sqrt(HD)
LOG2E = math.log2(math.e)

NT = (((1,), (1,)), ((), ()))
TN = (((0,), (0,)), ((), ()))
NN = (((1,), (0,)), ((), ()))

STAT_ROWS = 16
ATTEND_FLOPS = 10_000_000_000
SWAP = [(i, i ^ 1) for i in range(2 * CHIPS)]
NEIGHBOUR = [(i, i ^ 2) for i in range(2 * CHIPS)]
CLASSES = [
    [(x * SIDE + y) * 2 + core for x in range(SIDE) for y in rows]
    for core in range(2)
    for rows in ((0, 3), (1, 2))
]


def chip_shift(dx, dy):
    pairs = []
    for x in range(SIDE):
        for y in range(SIDE):
            target = ((x + dx) % SIDE) * SIDE + (y + dy) % SIDE
            for core in range(2):
                pairs.append(((x * SIDE + y) * 2 + core, target * 2 + core))
    return pairs


def head_shift(by):
    return [(i, (i + by) % HEADS) for i in range(HEADS)]


def swapped(value):
    return lax.ppermute(value, "seq", SWAP)


def neighboured(value):
    return lax.ppermute(value, "seq", NEIGHBOUR)


def vmem():
    return pl.BlockSpec(memory_space=pltpu.VMEM)


def smem():
    return pl.BlockSpec(memory_space=pltpu.SMEM)


def project_first(_near, own, forth_1, back_1, forth_2, back_2, weight, total_ref, later_ref, held, sems):
    me = lax.axis_index("head")
    depth = held.shape[2]
    offsets = (0, -1, 1, -2, 2, -3, 3, 4)

    def fetch(n):
        source = lax.rem(me + offsets[n] + HEADS, HEADS)
        columns = pl.ds(pl.multiple_of(source * depth, depth), depth)
        target = held.at[n] if n < 5 else later_ref.at[n - 5]
        return pltpu.make_async_copy(weight.at[:, columns], target, sems.at[n])

    for n in range(8):
        fetch(n).start()
    total = jnp.zeros(total_ref.shape, jnp.float32)
    for n, rows in enumerate((own, forth_1, back_1, forth_2, back_2)):
        fetch(n).wait()
        total += lax.dot_general(rows[...], held[n], NT, preferred_element_type=jnp.float32)
    total_ref[...] = total
    for n in range(5, 8):
        fetch(n).wait()


def project_last(
    _far, total_ref, forth_3, back_3, top, bottom, weight, attention_ref, norm_ref, grad_ref
):
    norms, deltas = [], []
    for slot, far in ((0, top), (1, bottom)):
        rows = slice(slot * HD, (slot + 1) * HD)
        total = total_ref[rows, :]
        for n, part in enumerate((forth_3[rows, :], back_3[rows, :], far[...])):
            total += lax.dot_general(part, weight[n], NT, preferred_element_type=jnp.float32)
        grad = total.astype(jnp.bfloat16)
        products = grad.astype(jnp.float32) * attention_ref[rows, :].astype(jnp.float32)
        for g in range(GROUP):
            columns = slice(g * HD, (g + 1) * HD)
            grad_ref[slot * STACK + g * HD : slot * STACK + (g + 1) * HD, :] = grad[:, columns]
            norms.append(norm_ref[g : g + 1, rows] * LOG2E)
            deltas.append(jnp.sum(jnp.transpose(products[:, columns]), axis=0, keepdims=True))
    rest = jnp.concatenate(norms + deltas, axis=0)
    for term in range(3):
        at = 2 * STACK + term * STAT_ROWS
        part = rest.astype(jnp.bfloat16)
        grad_ref[at : at + STAT_ROWS, :] = part
        rest = rest - part.astype(jnp.float32)


def plan(lengths, owners, position, slot, bound, place, target, before):
    me = lax.axis_index("seq")
    core = me & 1
    my_x, my_y = me >> 3, (me >> 1) & 3
    my_class = ((my_y + 1) >> 1) & 1

    def invert(i, carry):
        target[owners[i]] = i
        return carry

    lax.fori_loop(0, BLOCKS, invert, 0, unroll=8)

    def visit(t, n):
        row = jnp.where(t < SIDE_BLOCKS, 2 * t, 2 * (BLOCKS - 1 - t) + 1)
        goal = target[row]
        goal_y = (goal >> 2) & 3
        mine = (((goal >> 1) & 1) == core) & ((((goal_y + 1) >> 1) & 1) == my_class)
        before[t] = n
        position[n] = t
        slot[n] = (goal >> 4) * 4 + (goal_y >> 1) * 2 + (goal & 1)
        far = jnp.where(((row >> 1) & 1) == core, 0, SIDE_BLOCKS)
        back_x = (my_x - (row >> 4) + SIDE) & 3
        back_y = (my_y - ((row >> 2) & 3) + SIDE) & 3
        place[far + back_x * 8 + back_y * 2 + (row & 1)] = jnp.where(mine, n, MINE)
        return n + mine.astype(jnp.int32)

    before[BLOCKS] = lax.fori_loop(0, BLOCKS, visit, jnp.int32(0), unroll=8)
    position[MINE] = 4 * BLOCKS
    for q in range(8):
        device = me ^ (q >> 1)
        top = device if q % 2 == 0 else BLOCKS - 1 - device
        end = start = jnp.int32(0)
        for d in range(lengths.shape[0]):
            end = end + lengths[d]
            start = jnp.where(end <= top * HD, end, start)
        bound[2 * q] = before[start >> 7]
        bound[2 * q + 1] = before[top + 1]


def pack(keys, values, pair, sems):
    copies = [
        pltpu.make_async_copy(part, pair.at[:, n * HD : (n + 1) * HD], sems.at[n])
        for n, part in enumerate((keys, values))
    ]
    for copy in copies:
        copy.start()
    for copy in copies:
        copy.wait()


def hold(value, _dk, out):
    out[...] = value[...]


def tip(_bound, forth, back, top, bottom):
    top[...] = forth[:HD, :]
    bottom[...] = back[HD:, :]


def join(*refs):
    rows = refs[0].shape[0]
    for n in range(SIDE):
        refs[-1][n * rows : (n + 1) * rows, :] = refs[n][...]


def halve(forth, back, *refs):
    rows = refs[-1].shape[0]
    refs[-2][...] = forth[:rows, :]
    refs[-1][...] = back[rows:, :]


def sort_keys(place, *refs):
    pieces, (sorted_keys, sorted_values) = refs[:-2], refs[-2:]
    firsts = [side + first for side in (0, SIDE_BLOCKS) for first in (0, 8, 24, 16, 20)]
    goals = [place[n] for n in range(BLOCKS)]
    for first, piece in zip(firsts, pieces):
        for n in range(piece.shape[0] // HD):
            goal = pl.ds(pl.multiple_of(goals[first + n] * HD, HD), HD)
            rows = slice(n * HD, (n + 1) * HD)
            sorted_keys[goal, :] = piece[rows, :HD]
            sorted_values[goal, :] = piece[rows, HD:]
    for out in (sorted_keys, sorted_values):
        out[MINE * HD :, :] = jnp.zeros((HD, HD), jnp.bfloat16)


def visit_keys(
    away, lengths, position_ref, bound_ref, keys_ref, values_ref, queries, grads,
    dq_refs, dk_ref, dv_ref, dqt_ref, q_ref, do_ref,
):
    me = lax.axis_index("seq") ^ away
    upper = lax.broadcasted_iota(jnp.int32, (2 * HD, 1), 0)
    lane = lax.broadcasted_iota(jnp.int32, (1, 2 * STACK), 1)
    stats = []
    for ref in grads:
        terms = [
            ref[2 * STACK + n * STAT_ROWS : 2 * STACK + (n + 1) * STAT_ROWS, :].astype(jnp.float32)
            for n in range(3)
        ]
        stats.append((terms[2] + terms[1]) + terms[0])
    for slot in range(2):
        rows = slice(slot * HD, (slot + 1) * HD)
        for side in range(2):
            for g in range(GROUP):
                at = side * STACK + g * HD
                q_ref[at : at + HD, :] = queries[side][rows, g * HD : (g + 1) * HD]
            do_ref[side * STACK : (side + 1) * STACK, :] = grads[side][
                slot * STACK : (slot + 1) * STACK, :
            ]
        norm, delta = (
            jnp.concatenate(
                [
                    stats[side][kind * 8 + slot * GROUP + g : kind * 8 + slot * GROUP + g + 1, :]
                    for side in range(2)
                    for g in range(GROUP)
                ],
                axis=1,
            )
            for kind in range(2)
        )
        tops = [other if slot == 0 else BLOCKS - 1 - other for other in (me, me ^ 1)]
        last = jnp.where(lane < STACK, tops[0] * HD, tops[1] * HD) + (lane & (HD - 1))
        end = jnp.int32(0)
        first = jnp.zeros_like(last)
        for d in range(lengths.shape[0]):
            end = end + lengths[d]
            first = jnp.where(end <= last, end, first)
        at = 4 * away + 2 * slot
        begin = jnp.minimum(bound_ref[at], bound_ref[at + 4])
        stop = jnp.maximum(bound_ref[at + 1], bound_ref[at + 5])
        dqt_ref[...] = jnp.zeros_like(dqt_ref)

        def visit(step, carry):
            index = begin + 2 * step
            here = pl.ds(pl.multiple_of(index * HD, HD), 2 * HD)
            keys = keys_ref[here, :]
            queries = q_ref[...]
            grads = do_ref[...]
            low = position_ref[index] * HD
            high = (position_ref[index + 1] - 1) * HD
            place = upper + jnp.where(upper < HD, low, high)
            scores = lax.dot_general(keys, queries, NT, preferred_element_type=jnp.float32)
            prob_grad = lax.dot_general(
                values_ref[here, :], grads, NT, preferred_element_type=jnp.float32
            )
            allowed = (place >= first) & (place <= last)
            weights = jnp.where(allowed, jnp.exp2(scores * (FACTOR * LOG2E) - norm), 0.0)
            score_grad = (weights * (prob_grad - delta)).astype(jnp.bfloat16)
            dv_ref[here, :] += lax.dot_general(
                weights.astype(jnp.bfloat16), grads, NN, preferred_element_type=jnp.float32
            )
            dk_ref[here, :] += lax.dot_general(
                score_grad, queries, NN, preferred_element_type=jnp.float32
            )
            dqt_ref[...] += lax.dot_general(
                keys, score_grad, TN, preferred_element_type=jnp.float32
            )
            return carry

        lax.fori_loop(0, (stop - begin + 1) >> 1, visit, 0)
        for side in range(2):
            for g in range(GROUP):
                at = side * STACK + g * HD
                dq_refs[side][rows, g * HD : (g + 1) * HD] = (
                    jnp.transpose(dqt_ref[:, at : at + HD]) * FACTOR
                )


def attend_near(
    lengths, position, bound, keys, values, q_own, q_sib, grads_own, grads_sib,
    dk_ref, dv_ref, dq_own, dq_sib, *scratch,
):
    dk_ref[...] = jnp.zeros_like(dk_ref)
    dv_ref[...] = jnp.zeros_like(dv_ref)
    visit_keys(
        0, lengths, position, bound, keys, values, (q_own, q_sib), (grads_own, grads_sib),
        (dq_own, dq_sib), dk_ref, dv_ref, *scratch,
    )


def attend_far(
    lengths, position, slot_ref, bound, keys, values, q_near, q_far, grads_near, grads_far,
    dk_before, dv_before, parts_ref, dq_near, dq_far, dk_ref, dv_ref, *scratch,
):
    dk_ref[...] = dk_before[...]
    dv_ref[...] = dv_before[...]
    visit_keys(
        2, lengths, position, bound, keys, values, (q_near, q_far), (grads_near, grads_far),
        (dq_near, dq_far), dk_ref, dv_ref, *scratch,
    )

    def hand_out(n, carry):
        source = pl.ds(pl.multiple_of(n * HD, HD), HD)
        target = pl.ds(pl.multiple_of(slot_ref[n] * HD, HD), HD)
        parts_ref[target, :HD] = (dk_ref[source, :] * FACTOR).astype(jnp.bfloat16)
        parts_ref[target, HD:] = dv_ref[source, :].astype(jnp.bfloat16)
        return carry

    lax.fori_loop(0, MINE, hand_out, 0, unroll=2)


def anywhere():
    return pl.BlockSpec(memory_space=pl.ANY)


def array(shape, dtype):
    return jax.ShapeDtypeStruct(shape, dtype)


def call(body, outs, ins, out_specs, flops, moved, scratch=(), room=16):
    return pl.pallas_call(
        body,
        out_shape=outs,
        in_specs=ins,
        out_specs=out_specs,
        scratch_shapes=scratch,
        compiler_params=pltpu.CompilerParams(vmem_limit_bytes=room << 20),
        cost_estimate=pl.CostEstimate(flops=flops, bytes_accessed=moved, transcendentals=0),
        name=body.__name__,
    )


def per_device(
    query_heads,
    key_heads,
    value_heads,
    attention_out,
    log_norm,
    upstream,
    output_weight,
    document_lengths,
    block_owners,
):
    tokens, width = upstream.shape
    bf16, f32, i32 = jnp.bfloat16, jnp.float32, jnp.int32

    def along(axis, value, by):
        if axis == "z":
            return lax.ppermute(value, "head", head_shift(by))
        return lax.ppermute(value, "seq", chip_shift(by, 0) if axis == "x" else chip_shift(0, by))

    position, slot, bound, place = call(
        plan,
        (array((24,), i32), array((24,), i32), array((16,), i32), array((64,), i32)),
        [smem()] * 2,
        [smem()] * 4,
        0,
        1 << 20,
        [pltpu.SMEM((BLOCKS,), i32), pltpu.SMEM((BLOCKS + 8,), i32)],
    )(document_lengths, block_owners)

    pair = call(
        pack, array((tokens, 2 * HD), bf16), [anywhere()] * 2, vmem(), 0, 1 << 18,
        [pltpu.SemaphoreType.DMA((2,))],
    )(key_heads, value_heads)
    near = [pair, *[along("y", pair, by) for by in (1, 3, 2)]]
    forth, back = [upstream], [upstream]
    for _ in range(3):
        forth.append(along("z", forth[-1], 1))
        back.append(along("z", back[-1], -1))
    q_sib = swapped(query_heads)
    q_near = neighboured(query_heads)
    q_far = swapped(q_near)

    bundle_0 = call(
        join,
        array((SIDE * tokens, 2 * HD), bf16),
        [vmem()] * 4,
        vmem(),
        30_000_000_000,
        1 << 20,
    )(near[0], near[1], near[3], near[2])
    bundle_1, bundle_3 = along("x", bundle_0, 1), along("x", bundle_0, -1)

    total, later = call(
        project_first,
        (array((tokens, STACK), f32), array((3, STACK, width), bf16)),
        [anywhere()] + [vmem()] * 5 + [anywhere()],
        [vmem()] * 2,
        10_000_000_000,
        6 << 20,
        [pltpu.VMEM((5, STACK, width), bf16), pltpu.SemaphoreType.DMA((8,))],
    )(q_near, upstream, forth[1], back[1], forth[2], back[2], output_weight)

    half = array((SIDE * tokens // 2, 2 * HD), bf16)
    halves = call(
        halve, (half, half), [vmem()] * 2, [vmem()] * 2, 30_000_000_000, 1 << 20
    )(bundle_1, bundle_3)
    pieces = [bundle_0, bundle_1, bundle_3, along("x", halves[0], 1), along("x", halves[1], -1)]

    quarter = array((tokens // 2, width), bf16)
    tips = call(
        tip, (quarter, quarter), [smem()] + [vmem()] * 2, [vmem()] * 2, 0, 1 << 20
    )(bound, forth[3], back[3])
    top, bottom = along("z", tips[0], 1), along("z", tips[1], -1)
    grads = call(
        project_last,
        array((2 * STACK + 3 * STAT_ROWS, HD), bf16),
        [anywhere()] + [vmem()] * 8,
        vmem(),
        2 * tokens * 3 * width * STACK,
        3 << 20,
    )(q_far, total, forth[3], back[3], top, bottom, later, attention_out, log_norm)
    grads_sib = swapped(grads)
    grads_near = neighboured(grads)

    in_order = array(((MINE + 1) * HD, HD), bf16)
    keys, values = call(
        sort_keys, (in_order, in_order), [smem()] + [vmem()] * 10, [vmem()] * 2, 0, 6 << 20
    )(place, *pieces, *map(swapped, pieces))

    sums = array(((MINE + 1) * HD, HD), f32)
    rows_f32 = array((tokens, STACK), f32)
    scratch = [
        pltpu.VMEM((HD, 2 * STACK), f32),
        pltpu.VMEM((2 * STACK, HD), bf16),
        pltpu.VMEM((2 * STACK, HD), bf16),
    ]
    dk, dv, dq_own, dq_sib = call(
        attend_near,
        (sums, sums, rows_f32, rows_f32),
        [smem()] * 3 + [vmem()] * 6,
        [vmem()] * 4,
        100_000_000,
        4 << 20,
        scratch,
        24,
    )(document_lengths, position, bound, keys, values, query_heads, q_sib, grads, grads_sib)
    grads_near = call(
        hold, array(grads.shape, bf16), [vmem(), anywhere()], vmem(), 0, 1 << 20
    )(grads_near, dk)
    grads_far = swapped(grads_near)
    parts, dq_near, dq_far = call(
        attend_far,
        (array((MINE * HD, 2 * HD), bf16), rows_f32, rows_f32),
        [smem()] * 4 + [vmem()] * 8,
        [vmem()] * 3,
        ATTEND_FLOPS,
        4 << 20,
        [pltpu.VMEM(sums.shape, f32), pltpu.VMEM(sums.shape, f32), *scratch],
        24,
    )(
        document_lengths, position, slot, bound, keys, values, q_near, q_far,
        grads_near, grads_far, dk, dv,
    )
    returned = neighboured((dq_near + swapped(dq_far)).astype(bf16))
    query_grad = (dq_own + swapped(dq_sib) + returned.astype(f32)).astype(bf16)
    received = lax.all_to_all(
        parts.reshape(CHIPS // 2, 2 * HD, 2 * HD), "seq", 0, 0, tiled=True,
        axis_index_groups=CLASSES,
    )
    finished = jnp.sum(received.astype(f32), axis=0).astype(bf16)
    return (query_grad, finished[:, :HD], finished[:, HD:])


def solution(mesh):
    placed = (
        P("seq", "head"),
        P("seq", "head"),
        P("seq", "head"),
        P("seq", "head"),
        P("head", "seq"),
        P("seq", "head"),
        P("head", None),
        P(),
        P(),
    )
    return jax.shard_map(
        per_device,
        mesh=mesh,
        in_specs=placed,
        out_specs=(P("seq", "head"), P("seq", "head"), P("seq", "head")),
        check_vma=False,
    )
```

```python
import math

import jax
import jax.numpy as jnp
from jax import lax
from jax.experimental import pallas as pl
from jax.experimental.pallas import tpu as pltpu
from jax.sharding import PartitionSpec as P

HD = 128
GROUP = 4
SIDE = 4
CHIPS = SIDE * SIDE
HEADS = 8
BLOCKS = 64
SIDE_BLOCKS = BLOCKS // 2
MINE = BLOCKS // 4
STACK = GROUP * HD
FACTOR = 1.0 / math.sqrt(HD)
LOG2E = math.log2(math.e)

NT = (((1,), (1,)), ((), ()))
TN = (((0,), (0,)), ((), ()))
NN = (((1,), (0,)), ((), ()))

STAT_ROWS = 16
ATTEND_FLOPS = 10_000_000_000
SWAP = [(i, i ^ 1) for i in range(2 * CHIPS)]
NEIGHBOUR = [(i, i ^ 2) for i in range(2 * CHIPS)]
CLASSES = [
    [(x * SIDE + y) * 2 + core for x in range(SIDE) for y in rows]
    for core in range(2)
    for rows in ((0, 3), (1, 2))
]


def chip_shift(dx, dy):
    pairs = []
    for x in range(SIDE):
        for y in range(SIDE):
            target = ((x + dx) % SIDE) * SIDE + (y + dy) % SIDE
            for core in range(2):
                pairs.append(((x * SIDE + y) * 2 + core, target * 2 + core))
    return pairs


def head_shift(by):
    return [(i, (i + by) % HEADS) for i in range(HEADS)]


def swapped(value):
    return lax.ppermute(value, "seq", SWAP)


def neighboured(value):
    return lax.ppermute(value, "seq", NEIGHBOUR)


def vmem():
    return pl.BlockSpec(memory_space=pltpu.VMEM)


def smem():
    return pl.BlockSpec(memory_space=pltpu.SMEM)


def project_first(_near, own, forth_1, back_1, forth_2, back_2, weight, total_ref, later_ref, held, sems):
    me = lax.axis_index("head")
    depth = held.shape[2]
    offsets = (0, -1, 1, -2, 2, -3, 3, 4)

    def fetch(n):
        source = lax.rem(me + offsets[n] + HEADS, HEADS)
        columns = pl.ds(pl.multiple_of(source * depth, depth), depth)
        target = held.at[n] if n < 5 else later_ref.at[n - 5]
        return pltpu.make_async_copy(weight.at[:, columns], target, sems.at[n])

    for n in range(8):
        fetch(n).start()
    total = jnp.zeros(total_ref.shape, jnp.float32)
    for n, rows in enumerate((own, forth_1, back_1, forth_2, back_2)):
        fetch(n).wait()
        total += lax.dot_general(rows[...], held[n], NT, preferred_element_type=jnp.float32)
    total_ref[...] = total
    for n in range(5, 8):
        fetch(n).wait()


def project_last(
    _far, total_ref, forth_3, back_3, top, bottom, weight, attention_ref, norm_ref, grad_ref
):
    norms, deltas = [], []
    for slot, far in ((0, top), (1, bottom)):
        rows = slice(slot * HD, (slot + 1) * HD)
        total = total_ref[rows, :]
        for n, part in enumerate((forth_3[rows, :], back_3[rows, :], far[...])):
            total += lax.dot_general(part, weight[n], NT, preferred_element_type=jnp.float32)
        grad = total.astype(jnp.bfloat16)
        products = grad.astype(jnp.float32) * attention_ref[rows, :].astype(jnp.float32)
        for g in range(GROUP):
            columns = slice(g * HD, (g + 1) * HD)
            grad_ref[slot * STACK + g * HD : slot * STACK + (g + 1) * HD, :] = grad[:, columns]
            norms.append(norm_ref[g : g + 1, rows] * LOG2E)
            deltas.append(jnp.sum(jnp.transpose(products[:, columns]), axis=0, keepdims=True))
    rest = jnp.concatenate(norms + deltas, axis=0)
    for term in range(3):
        at = 2 * STACK + term * STAT_ROWS
        part = rest.astype(jnp.bfloat16)
        grad_ref[at : at + STAT_ROWS, :] = part
        rest = rest - part.astype(jnp.float32)


def plan(lengths, owners, position, slot, bound, place, target, before):
    me = lax.axis_index("seq")
    core = me & 1
    my_x, my_y = me >> 3, (me >> 1) & 3
    my_class = ((my_y + 1) >> 1) & 1

    def invert(i, carry):
        target[owners[i]] = i
        return carry

    lax.fori_loop(0, BLOCKS, invert, 0, unroll=BLOCKS)

    def visit(t, n):
        row = jnp.where(t < SIDE_BLOCKS, 2 * t, 2 * (BLOCKS - 1 - t) + 1)
        goal = target[row]
        goal_y = (goal >> 2) & 3
        mine = (((goal >> 1) & 1) == core) & ((((goal_y + 1) >> 1) & 1) == my_class)
        before[t] = n
        position[n] = t
        slot[n] = (goal >> 4) * 4 + (goal_y >> 1) * 2 + (goal & 1)
        far = jnp.where(((row >> 1) & 1) == core, 0, SIDE_BLOCKS)
        back_x = (my_x - (row >> 4) + SIDE) & 3
        back_y = (my_y - ((row >> 2) & 3) + SIDE) & 3
        place[far + back_x * 8 + back_y * 2 + (row & 1)] = jnp.where(mine, n, MINE)
        return n + mine.astype(jnp.int32)

    before[BLOCKS] = lax.fori_loop(0, BLOCKS, visit, jnp.int32(0), unroll=BLOCKS)
    for n in range(MINE, position.shape[0]):
        position[n] = 4 * BLOCKS
    for q in range(8):
        device = me ^ (q >> 1)
        top = device if q % 2 == 0 else BLOCKS - 1 - device
        end = start = jnp.int32(0)
        for d in range(lengths.shape[0]):
            end = end + lengths[d]
            start = jnp.where(end <= top * HD, end, start)
        bound[2 * q] = before[start >> 7]
        bound[2 * q + 1] = before[top + 1]


def hold(value, _dk, out):
    out[...] = value[...]


def hold_two(value, other, _keys, out, other_out):
    out[...] = value[...]
    other_out[...] = other[...]


def tip(_bound, forth, back, top, bottom):
    top[...] = forth[:HD, :]
    bottom[...] = back[HD:, :]


def join(*refs):
    rows = refs[0].shape[0]
    for n in range(SIDE):
        at = (SIDE - 1 - n) * rows
        refs[-1][at : at + rows, :] = refs[n][...]


def halve(back, forth, *refs):
    rows = refs[-1].shape[0]
    refs[-2][...] = forth[:rows, :]
    refs[-1][...] = back[rows:, :]


def place_blocks(place, firsts, pieces, sorted_keys, sorted_values):
    goals = [
        [place[first + n] for n in range(piece.shape[0] // HD)]
        for first, piece in zip(firsts, pieces)
    ]
    for spots, piece in zip(goals, pieces):
        for n, spot in enumerate(spots):
            goal = pl.ds(pl.multiple_of(spot * HD, HD), HD)
            rows = slice(n * HD, (n + 1) * HD)
            sorted_keys[goal, :] = piece[rows, :HD]
            sorted_values[goal, :] = piece[rows, HD:]


def sort_most(place, *refs):
    firsts = [side + first for side in (0, SIDE_BLOCKS) for first in (0, 8, 24)]
    place_blocks(place, firsts, refs[:-2], *refs[-2:])


def visit_keys(
    away, lengths, position_ref, bound_ref, keys_ref, values_ref, queries, grads,
    dqt_ref, dk_ref, dv_ref, q_ref, do_ref,
):
    me = lax.axis_index("seq") ^ away
    upper = lax.broadcasted_iota(jnp.int32, (2 * HD, 1), 0)
    lane = lax.broadcasted_iota(jnp.int32, (1, 2 * STACK), 1)
    stats = []
    for ref in grads:
        terms = [
            ref[2 * STACK + n * STAT_ROWS : 2 * STACK + (n + 1) * STAT_ROWS, :].astype(jnp.float32)
            for n in range(3)
        ]
        stats.append((terms[2] + terms[1]) + terms[0])
    for slot in range(2):
        rows = slice(slot * HD, (slot + 1) * HD)
        for side in range(2):
            for g in range(GROUP):
                at = side * STACK + g * HD
                q_ref[at : at + HD, :] = queries[side][rows, g * HD : (g + 1) * HD]
            do_ref[side * STACK : (side + 1) * STACK, :] = grads[side][
                slot * STACK : (slot + 1) * STACK, :
            ]
        norm, delta = (
            jnp.concatenate(
                [
                    stats[side][kind * 8 + slot * GROUP + g : kind * 8 + slot * GROUP + g + 1, :]
                    for side in range(2)
                    for g in range(GROUP)
                ],
                axis=1,
            )
            for kind in range(2)
        )
        tops = [other if slot == 0 else BLOCKS - 1 - other for other in (me, me ^ 1)]
        last = jnp.where(lane < STACK, tops[0] * HD, tops[1] * HD) + (lane & (HD - 1))
        end = jnp.int32(0)
        first = jnp.zeros_like(last)
        for d in range(lengths.shape[0]):
            end = end + lengths[d]
            first = jnp.where(end <= last, end, first)
        at = 4 * away + 2 * slot
        begin = jnp.minimum(bound_ref[at], bound_ref[at + 4])
        stop = jnp.maximum(bound_ref[at + 1], bound_ref[at + 5])
        dqt_ref[slot] = jnp.zeros(dqt_ref.shape[1:], jnp.float32)

        low_edge = jnp.int32(0)
        highest = jnp.maximum(tops[0], tops[1]) * HD + HD - 1
        end = jnp.int32(0)
        for d in range(lengths.shape[0]):
            end = end + lengths[d]
            low_edge = jnp.where(end <= highest, end, low_edge)
        high_block = jnp.minimum(tops[0], tops[1])

        def add(index, blocks, masked):
            here = pl.ds(pl.multiple_of(index * HD, HD), blocks * HD)
            keys = keys_ref[here, :]
            queries = q_ref[...]
            grads = do_ref[...]
            scores = lax.dot_general(keys, queries, NT, preferred_element_type=jnp.float32)
            prob_grad = lax.dot_general(
                values_ref[here, :], grads, NT, preferred_element_type=jnp.float32
            )
            weights = jnp.exp2(scores * (FACTOR * LOG2E) - norm)
            if masked:
                low = position_ref[index] * HD
                high = (position_ref[index + 1] - 1) * HD
                place = upper + jnp.where(upper < HD, low, high)
                weights = jnp.where((place >= first) & (place <= last), weights, 0.0)
            score_grad = (weights * (prob_grad - delta)).astype(jnp.bfloat16)
            dv_ref[here, :] += lax.dot_general(
                weights.astype(jnp.bfloat16), grads, NN, preferred_element_type=jnp.float32
            )
            dk_ref[here, :] += lax.dot_general(
                score_grad, queries, NN, preferred_element_type=jnp.float32
            )
            dqt_ref[slot] += lax.dot_general(
                keys, score_grad, TN, preferred_element_type=jnp.float32
            )

        def visit(index):
            after_edge = position_ref[index] * HD >= low_edge
            four = after_edge & (position_ref[index + 3] < high_block)

            @pl.when(four)
            def _():
                add(index, 4, False)

            @pl.when(jnp.logical_not(four))
            def _():
                add(index, 2, True)

            return index + jnp.where(four, 4, 2)

        lax.while_loop(lambda index: index < stop, visit, begin)


def attend_near(
    lengths, place, position, bound, half_0, half_1, half_2, half_3, _keys, _values,
    q_own, q_sib, grads_own, grads_sib, keys, values, dk_ref, dv_ref, dqt_ref, *scratch,
):
    firsts = [side + first for side in (0, SIDE_BLOCKS) for first in (16, 20)]
    place_blocks(place, firsts, (half_0, half_1, half_2, half_3), keys, values)
    for out in (keys, values):
        out[MINE * HD :, :] = jnp.zeros((HD, HD), jnp.bfloat16)
    dk_ref[...] = jnp.zeros_like(dk_ref)
    dv_ref[...] = jnp.zeros_like(dv_ref)
    visit_keys(
        0, lengths, position, bound, keys, values, (q_own, q_sib), (grads_own, grads_sib),
        dqt_ref, dk_ref, dv_ref, *scratch,
    )


def attend_far(
    lengths, position, slot_ref, bound, keys, values, q_near, q_far, grads_near, grads_far,
    _dk, _dv, parts_ref, dqt_ref, dk_ref, dv_ref, *scratch,
):
    visit_keys(
        2, lengths, position, bound, keys, values, (q_near, q_far), (grads_near, grads_far),
        dqt_ref, dk_ref, dv_ref, *scratch,
    )

    def hand_out(n, carry):
        source = pl.ds(pl.multiple_of(n * HD, HD), HD)
        target = pl.ds(pl.multiple_of(slot_ref[n] * HD, HD), HD)
        parts_ref[target, :HD] = (dk_ref[source, :] * FACTOR).astype(jnp.bfloat16)
        parts_ref[target, HD:] = dv_ref[source, :].astype(jnp.bfloat16)
        return carry

    lax.fori_loop(0, MINE, hand_out, 0, unroll=2)


def meet(near, far, out):
    out[...] = (near[:, :, :STACK] + far[...]).astype(jnp.bfloat16)


def finish(own, sibling, returned, out):
    for slot in range(2):
        total = own[slot, :, :STACK] + sibling[slot] + returned[slot].astype(jnp.float32)
        for g in range(GROUP):
            columns = slice(g * HD, (g + 1) * HD)
            out[slot * HD : (slot + 1) * HD, columns] = (
                jnp.transpose(total[:, columns]) * FACTOR
            ).astype(jnp.bfloat16)


def add_up(parts, key_grad, value_grad):
    for out, columns in ((key_grad, slice(0, HD)), (value_grad, slice(HD, 2 * HD))):
        total = parts[0, :, columns].astype(jnp.float32)
        for n in range(1, parts.shape[0]):
            total += parts[n, :, columns].astype(jnp.float32)
        out[...] = total.astype(jnp.bfloat16)


def anywhere():
    return pl.BlockSpec(memory_space=pl.ANY)


def array(shape, dtype):
    return jax.ShapeDtypeStruct(shape, dtype)


def call(body, outs, ins, out_specs, flops, moved, scratch=(), room=16, aliases=None):
    return pl.pallas_call(
        body,
        out_shape=outs,
        in_specs=ins,
        out_specs=out_specs,
        scratch_shapes=scratch,
        input_output_aliases=aliases or {},
        compiler_params=pltpu.CompilerParams(vmem_limit_bytes=room << 20),
        cost_estimate=pl.CostEstimate(flops=flops, bytes_accessed=moved, transcendentals=0),
        name=body.__name__,
    )


def per_device(
    query_heads,
    key_heads,
    value_heads,
    attention_out,
    log_norm,
    upstream,
    output_weight,
    document_lengths,
    block_owners,
):
    tokens, width = upstream.shape
    bf16, f32, i32 = jnp.bfloat16, jnp.float32, jnp.int32

    def along(axis, value, by):
        if axis == "z":
            return lax.ppermute(value, "head", head_shift(by))
        return lax.ppermute(value, "seq", chip_shift(by, 0) if axis == "x" else chip_shift(0, by))

    position, slot, bound, place = call(
        plan,
        (array((24,), i32), array((24,), i32), array((16,), i32), array((64,), i32)),
        [smem()] * 2,
        [smem()] * 4,
        0,
        1 << 20,
        [pltpu.SMEM((BLOCKS,), i32), pltpu.SMEM((BLOCKS + 8,), i32)],
    )(document_lengths, block_owners)

    pair = jnp.pad(key_heads, ((0, 0), (0, HD))) + jnp.pad(value_heads, ((0, 0), (HD, 0)))
    near = [*[along("y", pair, by) for by in (3, 2, 1)], pair]
    forth, back = [upstream], [upstream]
    for _ in range(3):
        forth.append(along("z", forth[-1], 1))
        back.append(along("z", back[-1], -1))
    q_sib = swapped(query_heads)
    q_near = neighboured(query_heads)
    q_far = swapped(q_near)

    bundle_0 = call(
        join,
        array((SIDE * tokens, 2 * HD), bf16),
        [vmem()] * 4,
        vmem(),
        30_000_000_000,
        1 << 20,
    )(*near)
    bundle_3, bundle_1 = along("x", bundle_0, -1), along("x", bundle_0, 1)

    total, later = call(
        project_first,
        (array((tokens, STACK), f32), array((3, STACK, width), bf16)),
        [anywhere()] + [vmem()] * 5 + [anywhere()],
        [vmem()] * 2,
        10_000_000_000,
        6 << 20,
        [pltpu.VMEM((5, STACK, width), bf16), pltpu.SemaphoreType.DMA((8,))],
    )(q_near, upstream, forth[1], back[1], forth[2], back[2], output_weight)

    half = array((SIDE * tokens // 2, 2 * HD), bf16)
    halves = call(
        halve, (half, half), [vmem()] * 2, [vmem()] * 2, 30_000_000_000, 1 << 20
    )(bundle_3, bundle_1)
    pieces = [bundle_0, bundle_1, bundle_3, along("x", halves[0], 1), along("x", halves[1], -1)]

    quarter = array((tokens // 2, width), bf16)
    tips = call(
        tip, (quarter, quarter), [anywhere()] + [vmem()] * 2, [vmem()] * 2, 0, 1 << 20
    )(bound, forth[3], back[3])
    top, bottom = along("z", tips[0], 1), along("z", tips[1], -1)
    grads = call(
        project_last,
        array((2 * STACK + 3 * STAT_ROWS, HD), bf16),
        [anywhere()] + [vmem()] * 8,
        vmem(),
        2 * tokens * 3 * width * STACK,
        3 << 20,
    )(q_far, total, forth[3], back[3], top, bottom, later, attention_out, log_norm)
    grads_sib = swapped(grads)
    grads_near = neighboured(grads)

    in_order = array(((MINE + 1) * HD, HD), bf16)
    most, rest = pieces[:3], pieces[3:]
    keys, values = call(
        sort_most, (in_order, in_order), [smem()] + [vmem()] * 6, [vmem()] * 2, 0, 4 << 20
    )(place, *most, *map(swapped, most))
    rest = call(
        hold_two, (half, half), [vmem()] * 2 + [anywhere()], [vmem()] * 2, 0, 1 << 20
    )(*rest, keys)
    sums = array(((MINE + 1) * HD, HD), f32)
    turned = array((2, HD, 2 * STACK), f32)
    scratch = [
        pltpu.VMEM((2 * STACK, HD), bf16),
        pltpu.VMEM((2 * STACK, HD), bf16),
    ]
    keys, values, dk, dv, dqt = call(
        attend_near,
        (in_order, in_order, sums, sums, turned),
        [smem()] * 4 + [vmem()] * 10,
        [vmem()] * 5,
        100_000_000,
        4 << 20,
        scratch,
        32,
        {8: 0, 9: 1},
    )(
        document_lengths, place, position, bound, *rest, *map(swapped, rest), keys, values,
        query_heads, q_sib, grads, grads_sib,
    )
    grads_near = call(
        hold, array(grads.shape, bf16), [vmem(), anywhere()], vmem(), 0, 1 << 20
    )(grads_near, dk)
    grads_far = swapped(grads_near)
    parts, dqt_away, _, _ = call(
        attend_far,
        (array((MINE * HD, 2 * HD), bf16), turned, sums, sums),
        [smem()] * 4 + [vmem()] * 8,
        [vmem()] * 4,
        ATTEND_FLOPS,
        4 << 20,
        scratch,
        32,
        {10: 2, 11: 3},
    )(
        document_lengths, position, slot, bound, keys, values, q_near, q_far,
        grads_near, grads_far, dk, dv,
    )
    half_turned = (2, HD, STACK)
    ours = call(
        meet, array(half_turned, bf16), [vmem()] * 2, vmem(), 0, 2 << 20
    )(dqt_away, swapped(dqt_away[:, :, STACK:]))
    query_grad = call(
        finish, array((tokens, STACK), bf16), [vmem()] * 3, vmem(), 0, 2 << 20
    )(dqt, swapped(dqt[:, :, STACK:]), neighboured(ours))
    received = lax.all_to_all(
        parts.reshape(CHIPS // 2, 2 * HD, 2 * HD), "seq", 0, 0, tiled=True,
        axis_index_groups=CLASSES,
    )
    local = array((tokens, HD), bf16)
    key_grad, value_grad = call(
        add_up, (local, local), [vmem()], [vmem()] * 2, 0, 1 << 20
    )(received)
    return (query_grad, key_grad, value_grad)


def solution(mesh):
    placed = (
        P("seq", "head"),
        P("seq", "head"),
        P("seq", "head"),
        P("seq", "head"),
        P("head", "seq"),
        P("seq", "head"),
        P("head", None),
        P(),
        P(),
    )
    return jax.shard_map(
        per_device,
        mesh=mesh,
        in_specs=placed,
        out_specs=(P("seq", "head"), P("seq", "head"), P("seq", "head")),
        check_vma=False,
    )
```

```python
import math

import jax
import jax.numpy as jnp
from jax import lax
from jax.experimental import pallas as pl
from jax.experimental.pallas import tpu as pltpu
from jax.sharding import PartitionSpec as P

HD = 128
GROUP = 4
SIDE = 4
CHIPS = SIDE * SIDE
HEADS = 8
BLOCKS = 64
SIDE_BLOCKS = BLOCKS // 2
MINE = BLOCKS // 4
STACK = GROUP * HD
FACTOR = 1.0 / math.sqrt(HD)
LOG2E = math.log2(math.e)

NT = (((1,), (1,)), ((), ()))
TN = (((0,), (0,)), ((), ()))
NN = (((1,), (0,)), ((), ()))

STAT_ROWS = 16
ATTEND_FLOPS = 10_000_000_000
SWAP = [(i, i ^ 1) for i in range(2 * CHIPS)]
NEIGHBOUR = [(i, i ^ 2) for i in range(2 * CHIPS)]
CLASSES = [
    [(x * SIDE + y) * 2 + core for x in range(SIDE) for y in rows]
    for core in range(2)
    for rows in ((0, 3), (1, 2))
]


def chip_shift(dx, dy):
    pairs = []
    for x in range(SIDE):
        for y in range(SIDE):
            target = ((x + dx) % SIDE) * SIDE + (y + dy) % SIDE
            for core in range(2):
                pairs.append(((x * SIDE + y) * 2 + core, target * 2 + core))
    return pairs


def head_shift(by):
    return [(i, (i + by) % HEADS) for i in range(HEADS)]


def swapped(value):
    return lax.ppermute(value, "seq", SWAP)


def neighboured(value):
    return lax.ppermute(value, "seq", NEIGHBOUR)


def vmem():
    return pl.BlockSpec(memory_space=pltpu.VMEM)


def smem():
    return pl.BlockSpec(memory_space=pltpu.SMEM)


def fetch(weight, slices, sems):
    me = lax.axis_index("head")
    depth = slices.shape[2]
    copies = []
    for n, offset in enumerate((0, -1, 1, -2, 2, -3, 3, 4)):
        source = lax.rem(me + offset + HEADS, HEADS)
        columns = pl.ds(pl.multiple_of(source * depth, depth), depth)
        copies.append(pltpu.make_async_copy(weight.at[:, columns], slices.at[n], sems.at[n]))
    for copy in copies:
        copy.start()
    for copy in copies:
        copy.wait()


def project_first(_near, own, forth_1, back_1, forth_2, back_2, weight, total_ref):
    total = jnp.zeros(total_ref.shape, jnp.float32)
    for n, rows in enumerate((own, forth_1, back_1, forth_2, back_2)):
        total += lax.dot_general(rows[...], weight[n], NT, preferred_element_type=jnp.float32)
    total_ref[...] = total


def project_last(
    _far, total_ref, forth_3, back_3, top, bottom, weight, attention_ref, norm_ref, grad_ref
):
    norms, deltas = [], []
    for slot, far in ((0, top), (1, bottom)):
        rows = slice(slot * HD, (slot + 1) * HD)
        total = total_ref[rows, :]
        for n, part in enumerate((forth_3[rows, :], back_3[rows, :], far[...])):
            total += lax.dot_general(part, weight[5 + n], NT, preferred_element_type=jnp.float32)
        grad = total.astype(jnp.bfloat16)
        products = grad.astype(jnp.float32) * attention_ref[rows, :].astype(jnp.float32)
        for g in range(GROUP):
            columns = slice(g * HD, (g + 1) * HD)
            grad_ref[slot * STACK + g * HD : slot * STACK + (g + 1) * HD, :] = grad[:, columns]
            norms.append(norm_ref[g : g + 1, rows] * LOG2E)
            deltas.append(jnp.sum(jnp.transpose(products[:, columns]), axis=0, keepdims=True))
    rest = jnp.concatenate(norms + deltas, axis=0)
    for term in range(3):
        at = 2 * STACK + term * STAT_ROWS
        part = rest.astype(jnp.bfloat16)
        grad_ref[at : at + STAT_ROWS, :] = part
        rest = rest - part.astype(jnp.float32)


def plan(lengths, owners, position, slot, bound, place, target, before):
    me = lax.axis_index("seq")
    core = me & 1
    my_x, my_y = me >> 3, (me >> 1) & 3
    my_class = ((my_y + 1) >> 1) & 1

    def invert(i, carry):
        target[owners[i]] = i
        return carry

    lax.fori_loop(0, BLOCKS, invert, 0, unroll=BLOCKS)

    def visit(t, n):
        row = jnp.where(t < SIDE_BLOCKS, 2 * t, 2 * (BLOCKS - 1 - t) + 1)
        goal = target[row]
        goal_y = (goal >> 2) & 3
        mine = (((goal >> 1) & 1) == core) & ((((goal_y + 1) >> 1) & 1) == my_class)
        before[t] = n
        position[n] = t
        slot[n] = (goal >> 4) * 4 + (goal_y >> 1) * 2 + (goal & 1)
        far = jnp.where(((row >> 1) & 1) == core, 0, SIDE_BLOCKS)
        back_x = (my_x - (row >> 4) + SIDE) & 3
        back_y = (my_y - ((row >> 2) & 3) + SIDE) & 3
        place[far + back_x * 8 + back_y * 2 + (row & 1)] = jnp.where(mine, n, MINE)
        return n + mine.astype(jnp.int32)

    before[BLOCKS] = lax.fori_loop(0, BLOCKS, visit, jnp.int32(0), unroll=BLOCKS)
    for n in range(MINE, position.shape[0]):
        position[n] = 4 * BLOCKS
    for q in range(8):
        device = me ^ (q >> 1)
        top = device if q % 2 == 0 else BLOCKS - 1 - device
        end = start = jnp.int32(0)
        for d in range(lengths.shape[0]):
            end = end + lengths[d]
            start = jnp.where(end <= top * HD, end, start)
        bound[2 * q] = before[start >> 7]
        bound[2 * q + 1] = before[top + 1]


def hold(value, _dk, out):
    out[...] = value[...]


def hold_two(value, other, _keys, out, other_out):
    out[...] = value[...]
    other_out[...] = other[...]


def tip(_bound, _slices, forth, back, top, bottom):
    top[...] = forth[:HD, :]
    bottom[...] = back[HD:, :]


def join(*refs):
    rows = refs[0].shape[0]
    for n in range(SIDE):
        at = (SIDE - 1 - n) * rows
        refs[-1][at : at + rows, :] = refs[n][...]


def halve(back, forth, *refs):
    rows = refs[-1].shape[0]
    refs[-2][...] = forth[:rows, :]
    refs[-1][...] = back[rows:, :]


def place_blocks(place, firsts, pieces, sorted_keys, sorted_values):
    goals = [
        [place[first + n] for n in range(piece.shape[0] // HD)]
        for first, piece in zip(firsts, pieces)
    ]
    for spots, piece in zip(goals, pieces):
        for n, spot in enumerate(spots):
            goal = pl.ds(pl.multiple_of(spot * HD, HD), HD)
            rows = slice(n * HD, (n + 1) * HD)
            sorted_keys[goal, :] = piece[rows, :HD]
            sorted_values[goal, :] = piece[rows, HD:]


def sort_most(place, *refs):
    firsts = [side + first for side in (0, SIDE_BLOCKS) for first in (0, 8, 24)]
    place_blocks(place, firsts, refs[:-2], *refs[-2:])


def visit_keys(
    away, lengths, position_ref, bound_ref, keys_ref, values_ref, queries, grads,
    dqt_ref, dk_ref, dv_ref, q_ref, do_ref,
):
    me = lax.axis_index("seq") ^ away
    upper = lax.broadcasted_iota(jnp.int32, (2 * HD, 1), 0)
    lane = lax.broadcasted_iota(jnp.int32, (1, 2 * STACK), 1)
    stats = []
    for ref in grads:
        terms = [
            ref[2 * STACK + n * STAT_ROWS : 2 * STACK + (n + 1) * STAT_ROWS, :].astype(jnp.float32)
            for n in range(3)
        ]
        stats.append((terms[2] + terms[1]) + terms[0])
    for slot in range(2):
        rows = slice(slot * HD, (slot + 1) * HD)
        for side in range(2):
            for g in range(GROUP):
                at = side * STACK + g * HD
                q_ref[at : at + HD, :] = queries[side][rows, g * HD : (g + 1) * HD]
            do_ref[side * STACK : (side + 1) * STACK, :] = grads[side][
                slot * STACK : (slot + 1) * STACK, :
            ]
        norm, delta = (
            jnp.concatenate(
                [
                    stats[side][kind * 8 + slot * GROUP + g : kind * 8 + slot * GROUP + g + 1, :]
                    for side in range(2)
                    for g in range(GROUP)
                ],
                axis=1,
            )
            for kind in range(2)
        )
        tops = [other if slot == 0 else BLOCKS - 1 - other for other in (me, me ^ 1)]
        last = jnp.where(lane < STACK, tops[0] * HD, tops[1] * HD) + (lane & (HD - 1))
        end = jnp.int32(0)
        first = jnp.zeros_like(last)
        for d in range(lengths.shape[0]):
            end = end + lengths[d]
            first = jnp.where(end <= last, end, first)
        at = 4 * away + 2 * slot
        begin = jnp.minimum(bound_ref[at], bound_ref[at + 4])
        stop = jnp.maximum(bound_ref[at + 1], bound_ref[at + 5])
        dqt_ref[slot] = jnp.zeros(dqt_ref.shape[1:], jnp.float32)

        low_edge = jnp.int32(0)
        highest = jnp.maximum(tops[0], tops[1]) * HD + HD - 1
        end = jnp.int32(0)
        for d in range(lengths.shape[0]):
            end = end + lengths[d]
            low_edge = jnp.where(end <= highest, end, low_edge)
        high_block = jnp.minimum(tops[0], tops[1])

        def add(index, blocks, masked):
            here = pl.ds(pl.multiple_of(index * HD, HD), blocks * HD)
            keys = keys_ref[here, :]
            queries = q_ref[...]
            grads = do_ref[...]
            scores = lax.dot_general(keys, queries, NT, preferred_element_type=jnp.float32)
            prob_grad = lax.dot_general(
                values_ref[here, :], grads, NT, preferred_element_type=jnp.float32
            )
            weights = jnp.exp2(scores * (FACTOR * LOG2E) - norm)
            if masked:
                low = position_ref[index] * HD
                high = (position_ref[index + 1] - 1) * HD
                place = upper + jnp.where(upper < HD, low, high)
                weights = jnp.where((place >= first) & (place <= last), weights, 0.0)
            score_grad = (weights * (prob_grad - delta)).astype(jnp.bfloat16)
            dv_ref[here, :] += lax.dot_general(
                weights.astype(jnp.bfloat16), grads, NN, preferred_element_type=jnp.float32
            )
            dk_ref[here, :] += lax.dot_general(
                score_grad, queries, NN, preferred_element_type=jnp.float32
            )
            dqt_ref[slot] += lax.dot_general(
                keys, score_grad, TN, preferred_element_type=jnp.float32
            )

        def visit(index):
            after_edge = position_ref[index] * HD >= low_edge
            four = after_edge & (position_ref[index + 3] < high_block)

            @pl.when(four)
            def _():
                add(index, 4, False)

            @pl.when(jnp.logical_not(four))
            def _():
                add(index, 2, True)

            return index + jnp.where(four, 4, 2)

        lax.while_loop(lambda index: index < stop, visit, begin)


def attend_near(
    lengths, place, position, bound, half_0, half_1, half_2, half_3, _keys, _values,
    q_own, q_sib, grads_own, grads_sib, keys, values, dk_ref, dv_ref, dqt_ref, *scratch,
):
    firsts = [side + first for side in (0, SIDE_BLOCKS) for first in (16, 20)]
    place_blocks(place, firsts, (half_0, half_1, half_2, half_3), keys, values)
    for out in (keys, values):
        out[MINE * HD :, :] = jnp.zeros((HD, HD), jnp.bfloat16)
    dk_ref[...] = jnp.zeros_like(dk_ref)
    dv_ref[...] = jnp.zeros_like(dv_ref)
    visit_keys(
        0, lengths, position, bound, keys, values, (q_own, q_sib), (grads_own, grads_sib),
        dqt_ref, dk_ref, dv_ref, *scratch,
    )


def attend_far(
    lengths, position, slot_ref, bound, keys, values, q_near, q_far, grads_near, grads_far,
    _dk, _dv, parts_ref, dqt_ref, dk_ref, dv_ref, *scratch,
):
    visit_keys(
        2, lengths, position, bound, keys, values, (q_near, q_far), (grads_near, grads_far),
        dqt_ref, dk_ref, dv_ref, *scratch,
    )

    def hand_out(n, carry):
        source = pl.ds(pl.multiple_of(n * HD, HD), HD)
        target = pl.ds(pl.multiple_of(slot_ref[n] * HD, HD), HD)
        parts_ref[target, :HD] = (dk_ref[source, :] * FACTOR).astype(jnp.bfloat16)
        parts_ref[target, HD:] = dv_ref[source, :].astype(jnp.bfloat16)
        return carry

    lax.fori_loop(0, MINE, hand_out, 0, unroll=2)


def meet(near, far, out):
    out[...] = (near[:, :, :STACK] + far[...]).astype(jnp.bfloat16)


def finish(own, sibling, returned, out):
    for slot in range(2):
        total = own[slot, :, :STACK] + sibling[slot] + returned[slot].astype(jnp.float32)
        for g in range(GROUP):
            columns = slice(g * HD, (g + 1) * HD)
            out[slot * HD : (slot + 1) * HD, columns] = (
                jnp.transpose(total[:, columns]) * FACTOR
            ).astype(jnp.bfloat16)


def add_up(parts, key_grad, value_grad):
    for out, columns in ((key_grad, slice(0, HD)), (value_grad, slice(HD, 2 * HD))):
        total = parts[0, :, columns].astype(jnp.float32)
        for n in range(1, parts.shape[0]):
            total += parts[n, :, columns].astype(jnp.float32)
        out[...] = total.astype(jnp.bfloat16)


def anywhere():
    return pl.BlockSpec(memory_space=pl.ANY)


def array(shape, dtype):
    return jax.ShapeDtypeStruct(shape, dtype)


def call(body, outs, ins, out_specs, flops, moved, scratch=(), room=16, aliases=None):
    return pl.pallas_call(
        body,
        out_shape=outs,
        in_specs=ins,
        out_specs=out_specs,
        scratch_shapes=scratch,
        input_output_aliases=aliases or {},
        compiler_params=pltpu.CompilerParams(vmem_limit_bytes=room << 20),
        cost_estimate=pl.CostEstimate(flops=flops, bytes_accessed=moved, transcendentals=0),
        name=body.__name__,
    )


def per_device(
    query_heads,
    key_heads,
    value_heads,
    attention_out,
    log_norm,
    upstream,
    output_weight,
    document_lengths,
    block_owners,
):
    tokens, width = upstream.shape
    bf16, f32, i32 = jnp.bfloat16, jnp.float32, jnp.int32

    def along(axis, value, by):
        if axis == "z":
            return lax.ppermute(value, "head", head_shift(by))
        return lax.ppermute(value, "seq", chip_shift(by, 0) if axis == "x" else chip_shift(0, by))

    position, slot, bound, place = call(
        plan,
        (array((24,), i32), array((24,), i32), array((16,), i32), array((64,), i32)),
        [smem()] * 2,
        [smem()] * 4,
        0,
        1 << 20,
        [pltpu.SMEM((BLOCKS,), i32), pltpu.SMEM((BLOCKS + 8,), i32)],
    )(document_lengths, block_owners)

    pair = jnp.pad(key_heads, ((0, 0), (0, HD))) + jnp.pad(value_heads, ((0, 0), (HD, 0)))
    near = [*[along("y", pair, by) for by in (3, 2, 1)], pair]
    forth, back = [upstream], [upstream]
    for _ in range(3):
        forth.append(along("z", forth[-1], 1))
        back.append(along("z", back[-1], -1))
    q_sib = swapped(query_heads)
    q_near = neighboured(query_heads)
    q_far = swapped(q_near)

    bundle_0 = call(
        join,
        array((SIDE * tokens, 2 * HD), bf16),
        [vmem()] * 4,
        vmem(),
        30_000_000_000,
        1 << 20,
    )(*near)
    bundle_3, bundle_1 = along("x", bundle_0, -1), along("x", bundle_0, 1)

    slices = call(
        fetch, array((HEADS, STACK, width), bf16), [anywhere()], vmem(), 0, 8 << 20,
        [pltpu.SemaphoreType.DMA((HEADS,))],
    )(output_weight)
    total = call(
        project_first,
        array((tokens, STACK), f32),
        [anywhere()] + [vmem()] * 6,
        vmem(),
        10_000_000_000,
        6 << 20,
    )(q_near, upstream, forth[1], back[1], forth[2], back[2], slices)

    half = array((SIDE * tokens // 2, 2 * HD), bf16)
    halves = call(
        halve, (half, half), [vmem()] * 2, [vmem()] * 2, 30_000_000_000, 1 << 20
    )(bundle_3, bundle_1)
    pieces = [bundle_0, bundle_1, bundle_3, along("x", halves[0], 1), along("x", halves[1], -1)]

    quarter = array((tokens // 2, width), bf16)
    tips = call(
        tip, (quarter, quarter), [anywhere()] * 2 + [vmem()] * 2, [vmem()] * 2, 0, 1 << 20
    )(bound, slices, forth[3], back[3])
    top, bottom = along("z", tips[0], 1), along("z", tips[1], -1)
    grads = call(
        project_last,
        array((2 * STACK + 3 * STAT_ROWS, HD), bf16),
        [anywhere()] + [vmem()] * 8,
        vmem(),
        2 * tokens * 3 * width * STACK,
        3 << 20,
    )(q_far, total, forth[3], back[3], top, bottom, slices, attention_out, log_norm)
    grads_sib = swapped(grads)
    grads_near = neighboured(grads)

    in_order = array(((MINE + 1) * HD, HD), bf16)
    most, rest = pieces[:3], pieces[3:]
    keys, values = call(
        sort_most, (in_order, in_order), [smem()] + [vmem()] * 6, [vmem()] * 2, 0, 4 << 20
    )(place, *most, *map(swapped, most))
    rest = call(
        hold_two, (half, half), [vmem()] * 2 + [anywhere()], [vmem()] * 2, 0, 1 << 20
    )(*rest, keys)
    sums = array(((MINE + 1) * HD, HD), f32)
    turned = array((2, HD, 2 * STACK), f32)
    scratch = [
        pltpu.VMEM((2 * STACK, HD), bf16),
        pltpu.VMEM((2 * STACK, HD), bf16),
    ]
    keys, values, dk, dv, dqt = call(
        attend_near,
        (in_order, in_order, sums, sums, turned),
        [smem()] * 4 + [vmem()] * 10,
        [vmem()] * 5,
        100_000_000,
        4 << 20,
        scratch,
        32,
        {8: 0, 9: 1},
    )(
        document_lengths, place, position, bound, *rest, *map(swapped, rest), keys, values,
        query_heads, q_sib, grads, grads_sib,
    )
    grads_near = call(
        hold, array(grads.shape, bf16), [vmem(), anywhere()], vmem(), 0, 1 << 20
    )(grads_near, dk)
    grads_far = swapped(grads_near)
    parts, dqt_away, _, _ = call(
        attend_far,
        (array((MINE * HD, 2 * HD), bf16), turned, sums, sums),
        [smem()] * 4 + [vmem()] * 8,
        [vmem()] * 4,
        ATTEND_FLOPS,
        4 << 20,
        scratch,
        32,
        {10: 2, 11: 3},
    )(
        document_lengths, position, slot, bound, keys, values, q_near, q_far,
        grads_near, grads_far, dk, dv,
    )
    half_turned = (2, HD, STACK)
    ours = call(
        meet, array(half_turned, bf16), [vmem()] * 2, vmem(), 0, 2 << 20
    )(dqt_away, swapped(dqt_away[:, :, STACK:]))
    query_grad = call(
        finish, array((tokens, STACK), bf16), [vmem()] * 3, vmem(), 0, 2 << 20
    )(dqt, swapped(dqt[:, :, STACK:]), neighboured(ours))
    received = lax.all_to_all(
        parts.reshape(CHIPS // 2, 2 * HD, 2 * HD), "seq", 0, 0, tiled=True,
        axis_index_groups=CLASSES,
    )
    local = array((tokens, HD), bf16)
    key_grad, value_grad = call(
        add_up, (local, local), [vmem()], [vmem()] * 2, 0, 1 << 20
    )(received)
    return (query_grad, key_grad, value_grad)


def solution(mesh):
    placed = (
        P("seq", "head"),
        P("seq", "head"),
        P("seq", "head"),
        P("seq", "head"),
        P("head", "seq"),
        P("seq", "head"),
        P("head", None),
        P(),
        P(),
    )
    return jax.shard_map(
        per_device,
        mesh=mesh,
        in_specs=placed,
        out_specs=(P("seq", "head"), P("seq", "head"), P("seq", "head")),
        check_vma=False,
    )
```
